256 devices in a mesh: slab: 64 (over z_lo, y, x, core), energy: 4 (over z_hi).
Axes of the slice: x: 4, y: 4, z: 8 (z_hi: 4, z_lo: 2; z = z_hi * 2 + z_lo), core: 2. Of those that a mesh axis runs over, the one named last changes fastest.
Arguments:
- green_blocks: float32 [512, 4, 2, 2, 128, 128], P('slab', 'energy'), may hold values from -1.1 to 1.1
- couplings: float32 [512, 128, 128], P('slab'), may hold values from -1.1 to 1.1
- green_cotangent: float32 [512, 4, 2, 2, 128, 128], P('slab', 'energy'), may hold values from -0.6 to 0.6
Outputs:
- onsite_grad: float32 [512, 128, 128], P('slab', 'energy')
- coupling_grad: float32 [512, 128, 128], P('slab', 'energy')
The draws below stay inside these ranges and needn't reach their ends.
All inputs are finite; a program needn't handle non-finite values.
Results may differ from the reference program's by a relative error of at most 0.0003.
Values sent between devices are 32-bit elements; how exact they have to be, the bound alone decides.
A program may use at most 128 MiB of HBM per device.

```python
import math
import jax
import jax.numpy as jnp
from jax import lax

B = 128
S_DEV = 8
WAVEVECTOR_COUNT = 2
LAYER_COUNT = 512
FREQUENCY_SAMPLE = 4


def draw_green_blocks(key, part):
    key = jax.random.fold_in(key, 11)
    common_seed, steady_seed, rapid_seed, rotation_seed, perturbation_seed, spike_seed = jax.random.split(key, 6)
    diag_shape = (LAYER_COUNT, FREQUENCY_SAMPLE, WAVEVECTOR_COUNT, B)
    full_shape = (LAYER_COUNT, FREQUENCY_SAMPLE, WAVEVECTOR_COUNT, 2, B, B)
    noise_scale = 0.6 / math.sqrt(2.0 * B * LAYER_COUNT)
    slow_tenths = 5
    fast_rate = jnp.exp(jax.random.uniform(rapid_seed, diag_shape, jnp.float32, 0.0, math.log(3.0))) / S_DEV
    noise = jnp.clip(jax.random.normal(perturbation_seed, full_shape, jnp.float32), -4.0, 4.0) * noise_scale
    slow_mask = (jax.random.randint(common_seed, (1, FREQUENCY_SAMPLE, WAVEVECTOR_COUNT, B), 0, 10) < slow_tenths).astype(jnp.float32)
    slow_rate = jax.random.uniform(steady_seed, (1, FREQUENCY_SAMPLE, WAVEVECTOR_COUNT, B), jnp.float32, 0.0, 0.4) / LAYER_COUNT
    rate = slow_mask * slow_rate + (1.0 - slow_mask) * fast_rate
    layer_positions = jax.random.randint(spike_seed, (FREQUENCY_SAMPLE, WAVEVECTOR_COUNT, 2), 0, LAYER_COUNT)
    hit = jnp.any(jnp.arange(LAYER_COUNT)[:, None, None, None] == layer_positions[None], axis=-1)
    factor = jnp.where(hit, 0.8, 1.0).astype(jnp.float32)[..., None]
    magnitude = jnp.exp(-rate) * factor
    phase = jax.random.uniform(rotation_seed, diag_shape, jnp.float32, -math.pi, math.pi)
    diagonal = jnp.stack([magnitude * jnp.cos(phase), magnitude * jnp.sin(phase)], axis=3)
    identity = (jnp.arange(B)[:, None] == jnp.arange(B)[None, :]).astype(jnp.float32)
    return noise + diagonal[..., :, None] * identity


def draw_couplings(key, part):
    key = jax.random.fold_in(key, 23)
    key_diag, perturbation_seed = jax.random.split(key, 2)
    noise_scale = 0.6 / math.sqrt(1.0 * B * LAYER_COUNT)
    hopping = jnp.exp(-jax.random.uniform(key_diag, (LAYER_COUNT, B), jnp.float32, 0.0, 0.2) / LAYER_COUNT)
    noise = jnp.clip(jax.random.normal(perturbation_seed, (LAYER_COUNT, B, B), jnp.float32), -4.0, 4.0) * noise_scale
    identity = (jnp.arange(B)[:, None] == jnp.arange(B)[None, :]).astype(jnp.float32)
    return noise * (1.0 - identity) + hopping[..., :, None] * identity


def steps_of(own_key, extent, cuts, low, high):
    level, own = 1.0, jax.random.fold_in(own_key, 6)
    for dim, shards_of in cuts:
        draws = jnp.exp(jax.random.uniform(jax.random.fold_in(own, dim), (shards_of,), jnp.float32, low / len(cuts), high / len(cuts)))
        level = level * jnp.repeat(draws, extent[dim] // shards_of).reshape([-1 if axis == dim else 1 for axis in range(len(extent))])
    return level


def bell_draw(own_key, extent, spread, bound, cuts=(), kind=jnp.bfloat16):
    drawn = spread * jax.random.normal(own_key, extent, jnp.float32)
    if cuts:
        drawn = drawn * steps_of(own_key, extent, cuts, -0.22, 0.18)
    return jnp.clip(drawn, -bound, bound).astype(kind)


def setup_inputs(seed: int = 0) -> dict:
    keys = jax.random.split(jax.random.key(seed), 4)
    green_blocks = draw_green_blocks(jax.random.fold_in(keys[3], 71), 0)
    couplings = draw_couplings(jax.random.fold_in(keys[3], 71), 0)
    green_cotangent = bell_draw(keys[2], (LAYER_COUNT, FREQUENCY_SAMPLE, WAVEVECTOR_COUNT, 2, B, B), 0.1, 0.6, ((0, 64), (1, 4)), jnp.float32)
    return {"green_blocks": green_blocks, "couplings": couplings, "green_cotangent": green_cotangent}


def matprod(left, right):
    return jnp.matmul(left, right, precision=lax.Precision.HIGHEST)


def complex_prod(left, right):
    left_re = left[..., 0, :, :]
    left_im = left[..., 1, :, :]
    right_re = right[..., 0, :, :]
    right_im = right[..., 1, :, :]
    return jnp.stack([matprod(left_re, right_re) - matprod(left_im, right_im), matprod(left_re, right_im) + matprod(left_im, right_re)], axis=-3)


def real_left(matrix, right):
    return jnp.stack([matprod(matrix, right[..., 0, :, :]), matprod(matrix, right[..., 1, :, :])], axis=-3)


def real_right(left, matrix):
    return jnp.stack([matprod(left[..., 0, :, :], matrix), matprod(left[..., 1, :, :], matrix)], axis=-3)


def flipped(value):
    return jnp.swapaxes(value, -1, -2)


def reference(green_blocks, couplings, green_cotangent):
    def one_slab(carried, inputs):
        adjoint_next, green_next, weight_next = carried
        cotangent, green_now, coupling_now = inputs
        linkage = real_left(coupling_now, flipped(green_next))
        adjoint_now = cotangent + complex_prod(complex_prod(linkage, adjoint_next), flipped(linkage))
        weight_now = complex_prod(complex_prod(flipped(green_now), adjoint_now), flipped(green_now))
        onsite = jnp.sum(weight_now[..., 0, :, :], axis=(0, 1))
        forward_part = complex_prod(real_right(green_now, coupling_now), flipped(weight_next))
        backward_part = complex_prod(real_right(flipped(green_now), coupling_now), weight_next)
        coupling = jnp.sum((forward_part + backward_part)[..., 0, :, :], axis=(0, 1))
        return (adjoint_now, green_now, weight_now), (onsite, coupling)

    zeros = jnp.zeros(green_blocks.shape[1:], green_blocks.dtype)
    _, (onsite_grad, coupling_grad) = lax.scan(one_slab, (zeros, zeros, zeros), (green_cotangent, green_blocks, couplings), reverse=True)
    return onsite_grad, coupling_grad
```

```python
import functools

import jax
import jax.numpy as jnp
from jax import lax
from jax.experimental import pallas as pl
from jax.experimental.pallas import tpu as pltpu
from jax.sharding import PartitionSpec as P

F32 = jnp.float32
BF16 = jnp.bfloat16
MESH = pl.DeviceIdType.MESH
B = 128
S = 8
ROWS = 32
NX, NY = 4, 4


def split(a):
    high = a.astype(BF16)
    return high, (a - high.astype(F32)).astype(BF16)


def dot(a, b, nt=False):
    return lax.dot_general(
        a, b, (((1,), (1 if nt else 0,)), ((), ())), preferred_element_type=F32
    )


def wide(b):
    re, im = b[:, :B], b[:, B:]
    return jnp.concatenate([b, jnp.concatenate([-im, re], 1)], 0)


def wide_t(b):
    re, im = b[:, :B], b[:, B:]
    return jnp.concatenate(
        [jnp.concatenate([re, -im], 1), jnp.concatenate([im, re], 1)], 0
    )


def lhs(x):
    high, low = split(x)
    return jnp.concatenate([high, low], 0)


def rhs(b):
    high, low = split(b)
    return wide(high), wide(low)


def rhs_t(b):
    high, low = split(b)
    return wide_t(high), wide_t(low)


def mul(x, w, nt=False):
    rows = x.shape[0] // 2
    y = dot(x, w[0], nt)
    return y[:rows] + y[rows:] + dot(x[:rows], w[1], nt)


def apply_map(off, prod, inner):
    return off + mul(lhs(mul(lhs(prod), rhs(inner))), rhs_t(prod), True)


def combine(first, second):
    off1, p1 = first
    off2, p2 = second
    left = lhs(p1)
    y = mul(left, rhs(off2))
    prod = mul(left, rhs(p2))
    return off1 + mul(lhs(y), rhs_t(p1), True), prod


def kernel(
    g_hbm, u_hbm, c_hbm, on_ref, cp_ref,
    g, u, c, link, own, tbuf, xs, ys, ex, ey, zbuf, dbuf, zrecv, xin,
    ap, gt, w0, q, gg, vv, xt, w, part, recv,
    in_sem, halo_sem, pair_sem, x_send, x_recv, y_send, y_recv, z_sem, d_sem, r_send, r_recv,
):
    s = lax.axis_index("slab")
    e = lax.axis_index("energy")
    core = lax.rem(s, 2)
    x = lax.rem(s // 2, NX)
    y = lax.rem(s // (2 * NX), NY)
    z = s // (2 * NX * NY)
    slabs = 2 * NX * NY * 2
    prev = lax.rem(s + slabs - 1, slabs)
    after = lax.rem(s + 1, slabs)
    partner = s + 1 - 2 * core
    zpeer = lax.rem(s + slabs // 2, slabs)

    def xpeer(d):
        return s + (lax.rem(x + d, NX) - x) * 2

    def ypeer(d):
        return s + (lax.rem(y + d, NY) - y) * (2 * NX)

    def epeer(d):
        return lax.rem(e + d, 4)

    cg = pltpu.make_async_copy(g_hbm, g.at[pl.ds(0, S)], in_sem.at[0])
    cu = pltpu.make_async_copy(u_hbm, u, in_sem.at[1])
    cc = pltpu.make_async_copy(c_hbm, c, in_sem.at[2])
    cg.start()
    cu.start()
    cc.start()

    barrier = pltpu.get_barrier_semaphore()
    greet = [(prev, e), (after, e), (partner, e), (zpeer, e)]
    greet += [(xpeer(d), e) for d in (1, 2, 3)]
    greet += [(ypeer(d), e) for d in (1, 2, 3)]
    greet += [(s, epeer(d)) for d in (1, 2, 3)]
    for device in greet:
        pl.semaphore_signal(barrier, inc=1, device_id=device, device_id_type=MESH)
    pl.semaphore_wait(barrier, len(greet))

    def remote(src, dst, send, recv_, device):
        return pltpu.make_async_remote_copy(
            src_ref=src, dst_ref=dst, send_sem=send, recv_sem=recv_,
            device_id=device, device_id_type=MESH,
        )

    halo = remote(g_hbm.at[0], g.at[S], halo_sem.at[0], halo_sem.at[1], (prev, e))
    halo.start()

    def cat(ref, i, k):
        return jnp.concatenate([ref[i, k, 0], ref[i, k, 1]], 1)

    def make_links(i, scale=None):
        ui = u[i]
        if scale is not None:
            ui = ui * scale
        uu = lhs(ui)
        out = []
        for k in range(2):
            gh, gl = split(jnp.concatenate([g[i + 1, k, 0], g[i + 1, k, 1]], 0))
            value = mul(uu, (gh, gl), True)
            link[i, k] = value
            out.append(value)
        return out

    cg.wait()
    cu.wait()
    first = make_links(0)
    cc.wait()
    for k in range(2):
        own[k, 0] = cat(c, 0, k)
        own[k, 1] = first[k]

    def fold(i, carry):
        links = make_links(i)
        for k in range(2):
            pk = own[k, 1]
            left = lhs(pk)
            yk = mul(left, rhs(cat(c, i, k)))
            own[k, 1] = mul(left, rhs(links[k]))
            own[k, 0] += mul(lhs(yk), rhs_t(pk), True)
        return carry

    lax.fori_loop(1, S - 1, fold, 0)
    halo.wait_recv()
    links = make_links(S - 1, jnp.where(s == slabs - 1, 0.0, 1.0).astype(F32))
    for k in range(2):
        pk = own[k, 1]
        left = lhs(pk)
        yk = mul(left, rhs(cat(c, S - 1, k)))
        own[k, 1] = mul(left, rhs(links[k]))
        own[k, 0] += mul(lhs(yk), rhs_t(pk), True)

    pair = remote(
        own.at[1 - core], tbuf.at[core], pair_sem.at[0], pair_sem.at[1], (partner, e)
    )
    pair.start()
    tbuf[core] = own[core]
    pair.wait_recv()

    def both(ref, i):
        return ref[i, 0], ref[i, 1]

    def put(ref, i, value):
        ref[i, 0] = value[0]
        ref[i, 1] = value[1]

    put(xs, x, combine(both(tbuf, 0), both(tbuf, 1)))

    def gather(ref, me, peer, send, recv_):
        out = []
        for d in (1, 2, 3):
            copy = remote(
                ref.at[me], ref.at[me], send.at[d - 1], recv_.at[d - 1], (peer(d), e)
            )
            copy.start()
            out.append(copy)
        return out

    x_copies = gather(xs, x, xpeer, x_send, x_recv)

    def flip(i):
        for k in range(2):
            gt[i, k] = jnp.concatenate([g[i, k, 0].T, g[i, k, 1].T], 1)

    def prepare(i):
        flip(i)
        uh, ul = split(u[i])
        uu = jnp.concatenate([uh, ul], 1)
        for k in range(2):
            a0, ps = ap[k, 0], ap[k, 1]
            gi, gti = cat(g, i, k), gt[i, k]
            lg = lhs(gi)
            lt = lhs(gti)
            h0 = mul(lt, rhs(a0))
            w0[i, k] = mul(lhs(h0), rhs(gti))
            pw = rhs(ps)
            q[i, k] = lhs(mul(lt, pw))
            gg[i, k] = mul(lg, pw)
            rows = [gi[:, :B], -gi[:, B:], gti[:, :B], -gti[:, B:]]
            xh, xl = split(jnp.concatenate(rows, 0))
            t = dot(xh, uu)
            vh, vl = split(t[:, :B] + t[:, B:] + dot(xl, uh))
            for n in range(4):
                column = (n // 2) * 512 + k * 256 + (n % 2) * B
                vv[i, 0:B, column : column + B] = vh[n * B : n * B + B]
                vv[i, B : 2 * B, column : column + B] = vl[n * B : n * B + B]

    def step_back(i):
        for k in range(2):
            lk = link[i, k]
            left = lhs(lk)
            yk = mul(left, rhs(ap[k, 0]))
            pk = mul(left, rhs(ap[k, 1]))
            ap[k, 1] = pk
            ap[k, 0] = cat(c, i, k) + mul(lhs(yk), rhs_t(lk), True)

    for k in range(2):
        ap[k, 0] = cat(c, S - 1, k)
        ap[k, 1] = link[S - 1, k]
    flip(S)
    for k in range(2):
        w0[S, k] = jnp.zeros((B, 2 * B), F32)
        q[S, k] = lhs(gt[S, k])
        gg[S, k] = cat(g, S, k)
    prepare(S - 1)

    def shadow(j, carry):
        i = S - 2 - j
        step_back(i)
        prepare(i)
        return carry

    lax.fori_loop(0, 3, shadow, 0)

    def finish(copies):
        for copy in copies:
            copy.wait_recv()

    def level_total(ref):
        t01 = combine(both(ref, 0), both(ref, 1))
        t23 = combine(both(ref, 2), both(ref, 3))
        return t23, combine(t01, t23)

    row_i = lax.broadcasted_iota(jnp.int32, (B, 2 * B), 0)
    col_i = lax.broadcasted_iota(jnp.int32, (B, 2 * B), 1)
    unit = jnp.where(row_i == col_i, 1.0, 0.0).astype(F32)

    def later(ref, out, t23):
        put(out, 0, combine(both(ref, 1), t23))
        put(out, 1, t23)
        out[2] = ref[3]
        out[3, 0] = jnp.zeros((B, 2 * B), F32)
        out[3, 1] = unit

    finish(x_copies)
    t23, total = level_total(xs)
    put(ys, y, total)
    y_copies = gather(ys, y, ypeer, y_send, y_recv)
    later(xs, ex, t23)
    lax.fori_loop(3, S - 1, shadow, 0)

    finish(y_copies)
    t23, total = level_total(ys)
    zbuf[...] = total[0]
    zcopy = remote(zbuf, zrecv, z_sem.at[0], z_sem.at[1], (zpeer, e))

    @pl.when(z == 1)
    def _():
        zcopy.start()
        zrecv[...] = jnp.zeros((B, 2 * B), F32)

    later(ys, ey, t23)
    outer = combine(both(ex, x), both(ey, y))
    inner = combine(both(tbuf, 1), outer)

    @pl.when(z == 0)
    def _():
        zcopy.wait_recv()

    top = zrecv[...]
    chip_in = apply_map(outer[0], outer[1], top)
    core_in = apply_map(inner[0], inner[1], top)
    is_first = core == 0
    dbuf[...] = jnp.where(is_first, chip_in, core_in)
    down = remote(dbuf, xin.at[core], d_sem.at[0], d_sem.at[1], (partner, e))
    down.start()
    xin[core] = jnp.where(is_first, core_in, chip_in)
    down.wait_recv()

    for k in range(2):
        high, low = rhs(xin[k])
        xt[k, 0] = high
        xt[k, 1] = low

    def weights(i):
        for k in range(2):
            zk = mul(q[i, k], (xt[k, 0], xt[k, 1]))
            w[i, k] = w0[i, k] + mul(lhs(zk), rhs_t(gg[i, k]), True)

    weights(S)

    def finals(j, carry):
        i = S - 1 - j
        wh0, wl0 = split(w[i + 1, 0])
        wh1, wl1 = split(w[i + 1, 1])
        nt = jnp.concatenate(
            [jnp.concatenate([wh0, wh1], 1), jnp.concatenate([wl0, wl1], 1)], 0
        )
        nn = jnp.concatenate(
            [
                jnp.concatenate([h[:, m : m + B], l[:, m : m + B]], 1)
                for h, l in ((wh0, wl0), (wh1, wl1))
                for m in (0, B)
            ],
            0,
        )
        t = dot(vv[i, :, 0:512], nt, True) + dot(vv[i, :, 512:1024], nn)
        coupling = t[:B, :B] + (t[:B, B:] + t[B:, :B])
        weights(i)
        onsite = w[i, 0, :, 0:B] + w[i, 1, :, 0:B]
        for r in range(4):
            part[i, r, 0] = onsite[r * ROWS : (r + 1) * ROWS]
            part[i, r, 1] = coupling[r * ROWS : (r + 1) * ROWS]
        for d in (1, 2, 3):
            spread(i, d).start()
        return carry

    def spread(i, d):
        return remote(
            part.at[i, epeer(d)], recv.at[i, d - 1],
            r_send.at[i, d - 1], r_recv.at[i, d - 1], (s, epeer(d)),
        )

    lax.fori_loop(0, S, finals, 0)

    def collect(j, carry):
        i = S - 1 - j
        for d in (1, 2, 3):
            spread(i, d).wait_recv()
        total_i = part[i, e] + recv[i, 0] + (recv[i, 1] + recv[i, 2])
        on_ref[i] = total_i[0]
        cp_ref[i] = total_i[1]
        return carry

    lax.fori_loop(0, S, collect, 0)

    halo.wait_send()
    pair.wait_send()
    for copy in x_copies + y_copies:
        copy.wait_send()

    @pl.when(z == 1)
    def _():
        zcopy.wait_send()

    down.wait_send()

    def drain(i, carry):
        for d in (1, 2, 3):
            spread(i, d).wait_send()
        return carry

    lax.fori_loop(0, S, drain, 0)


def on_device(green_blocks, couplings, green_cotangent):
    shape = (S, 2, 2, B, B)
    block = (B, 2 * B)
    vmem = pltpu.VMEM
    out = jax.ShapeDtypeStruct((S, ROWS, B), F32)
    dma = pltpu.SemaphoreType.DMA
    return pl.pallas_call(
        kernel,
        out_shape=(out, out),
        in_specs=[pl.BlockSpec(memory_space=pl.ANY)] * 3,
        out_specs=(pl.BlockSpec(memory_space=vmem),) * 2,
        scratch_shapes=[
            vmem((S + 1, 2, 2, B, B), F32),
            vmem((S, B, B), F32),
            vmem(shape, F32),
            vmem((S, 2) + block, F32),
            vmem((2, 2) + block, F32),
            vmem((2, 2) + block, F32),
            vmem((NX, 2) + block, F32),
            vmem((NY, 2) + block, F32),
            vmem((NX, 2) + block, F32),
            vmem((NY, 2) + block, F32),
            vmem(block, F32),
            vmem(block, F32),
            vmem(block, F32),
            vmem((2,) + block, F32),
            vmem((2, 2) + block, F32),
            vmem((S + 1, 2) + block, F32),
            vmem((S + 1, 2) + block, F32),
            vmem((S + 1, 2, 2 * B, 2 * B), BF16),
            vmem((S + 1, 2) + block, F32),
            vmem((S, 2 * B, 8 * B), BF16),
            vmem((2, 2, 2 * B, 2 * B), BF16),
            vmem((S + 1, 2) + block, F32),
            vmem((S, 4, 2, ROWS, B), F32),
            vmem((S, 3, 2, ROWS, B), F32),
            dma((3,)),
            dma((2,)),
            dma((2,)),
            dma((3,)),
            dma((3,)),
            dma((3,)),
            dma((3,)),
            dma((2,)),
            dma((2,)),
            dma((S, 3)),
            dma((S, 3)),
        ],
        compiler_params=pltpu.CompilerParams(
            collective_id=0, has_side_effects=True, vmem_limit_bytes=50 * 1024 * 1024
        ),
    )(
        green_blocks.reshape(shape),
        couplings,
        green_cotangent.reshape(shape),
    )


def solution(mesh):
    in_specs = (
        P("slab", "energy", None, None, None, None),
        P("slab", None, None),
        P("slab", "energy", None, None, None, None),
    )
    out_specs = (P("slab", "energy", None), P("slab", "energy", None))
    return jax.shard_map(
        on_device, mesh=mesh, in_specs=in_specs, out_specs=out_specs, check_vma=False
    )
```

```python
import functools

import jax
import jax.numpy as jnp
from jax import lax
from jax.experimental import pallas as pl
from jax.experimental.pallas import tpu as pltpu
from jax.sharding import PartitionSpec as P

F32 = jnp.float32
BF16 = jnp.bfloat16
MESH = pl.DeviceIdType.MESH
B = 128
S = 8
ROWS = 32
NX, NY = 4, 4


def split(a):
    high = a.astype(BF16)
    return high, (a - high.astype(F32)).astype(BF16)


def dot(a, b, nt=False):
    return lax.dot_general(
        a, b, (((1,), (1 if nt else 0,)), ((), ())), preferred_element_type=F32
    )


def wide(b):
    re, im = b[:, :B], b[:, B:]
    return jnp.concatenate([b, jnp.concatenate([-im, re], 1)], 0)


def wide_t(b):
    re, im = b[:, :B], b[:, B:]
    return jnp.concatenate(
        [jnp.concatenate([re, -im], 1), jnp.concatenate([im, re], 1)], 0
    )


def lhs(x):
    high, low = split(x)
    return jnp.concatenate([high, low], 0)


def rhs(b):
    high, low = split(b)
    return wide(high), wide(low)


def rhs_t(b):
    high, low = split(b)
    return wide_t(high), wide_t(low)


def mul(x, w, nt=False):
    rows = x.shape[0] // 2
    y = dot(x, w[0], nt)
    return y[:rows] + y[rows:] + dot(x[:rows], w[1], nt)


def apply_map(off, prod, inner):
    return off + mul(lhs(mul(lhs(prod), rhs(inner))), rhs_t(prod), True)


def combine(first, second):
    off1, p1 = first
    off2, p2 = second
    left = lhs(p1)
    y = mul(left, rhs(off2))
    prod = mul(left, rhs(p2))
    return off1 + mul(lhs(y), rhs_t(p1), True), prod


def kernel(
    g_hbm, u_hbm, c_hbm, on_ref, cp_ref,
    g, u, c, link, pre, own, tbuf, xs, ys, ex, ey, lp, lo, zbuf, dbuf, zrecv, xin,
    ap, gt, w0, q, gg, vv, xt, w, part, relay, recv,
    g_sem, in_sem, pair_sem, x_send, x_recv, y_send, y_recv, z_sem, d_sem, h_sem,
    r_send, r_recv,
):
    s = lax.axis_index("slab")
    e = lax.axis_index("energy")
    core = lax.rem(s, 2)
    x = lax.rem(s // 2, NX)
    y = lax.rem(s // (2 * NX), NY)
    z = s // (2 * NX * NY)
    slabs = 2 * NX * NY * 2
    prev = lax.rem(s + slabs - 1, slabs)
    after = lax.rem(s + 1, slabs)
    partner = s + 1 - 2 * core
    zpeer = lax.rem(s + slabs // 2, slabs)
    last = s == slabs - 1

    def xpeer(d):
        return s + (lax.rem(x + d, NX) - x) * 2

    def ypeer(d):
        return s + (lax.rem(y + d, NY) - y) * (2 * NX)

    def epeer(d):
        return lax.rem(e + d, 4)

    barrier = pltpu.get_barrier_semaphore()
    greet = [(prev, e), (after, e), (partner, e), (zpeer, e)]
    greet += [(xpeer(d), e) for d in (1, 3)]
    greet += [(ypeer(d), e) for d in (1, 3)]
    greet += [(s, epeer(d)) for d in (1, 3)]
    for device in greet:
        pl.semaphore_signal(barrier, inc=1, device_id=device, device_id_type=MESH)

    def g_copy(i):
        return pltpu.make_async_copy(g_hbm.at[i], g.at[i], g_sem.at[i])

    cu = pltpu.make_async_copy(u_hbm, u, in_sem.at[0])
    cc = pltpu.make_async_copy(c_hbm, c, in_sem.at[1])
    g_copy(0).start()
    cu.start()
    for i in range(1, S):
        g_copy(i).start()
    cc.start()

    def remote(src, dst, send, recv_, device):
        return pltpu.make_async_remote_copy(
            src_ref=src, dst_ref=dst, send_sem=send, recv_sem=recv_,
            device_id=device, device_id_type=MESH,
        )

    def cat(ref, i, k):
        return jnp.concatenate([ref[i, k, 0], ref[i, k, 1]], 1)

    def flip(i):
        for k in range(2):
            gt[i, k] = jnp.concatenate([g[i, k, 0].T, g[i, k, 1].T], 1)

    g_copy(0).wait()
    flip(0)
    for k in range(2):
        pre[0, k] = gt[0, k]
    cu.wait()

    def chain(i, carry):
        g_copy(i + 1).wait()
        uu = lhs(u[i])
        for k in range(2):
            gh, gl = split(jnp.concatenate([g[i + 1, k, 0], g[i + 1, k, 1]], 0))
            value = mul(uu, (gh, gl), True)
            link[i, k] = value
            pre[i + 1, k] = mul(lhs(pre[i, k]), rhs(value))
        return carry

    lax.fori_loop(0, S - 1, chain, 0)
    last_u = u[S - 1] * jnp.where(last, 0.0, 1.0).astype(F32)
    uw = split(last_u)
    for k in range(2):
        value = pre[S - 1, k]
        t = mul(lhs(jnp.concatenate([value[:, :B], value[:, B:]], 0)), uw)
        own[k, 1] = jnp.concatenate([t[:B], t[B:]], 1)

    pl.semaphore_wait(barrier, len(greet))

    def pair(t):
        return remote(
            own.at[1 - core, t], tbuf.at[core, t],
            pair_sem.at[0, t], pair_sem.at[1, t], (partner, e),
        )

    pair(1).start()
    tbuf[core, 1] = own[core, 1]
    cc.wait()
    for k in range(2):
        own[k, 0] = jnp.zeros((B, 2 * B), F32)

    def fold(i, carry):
        for k in range(2):
            pk = pre[i, k]
            yk = mul(lhs(pk), rhs(cat(c, i, k)))
            own[k, 0] += mul(lhs(yk), rhs_t(pk), True)
        return carry

    class Ring:
        def __init__(self, ref, t, me, peer, send, recv_):
            self.ref, self.t, self.me, self.peer = ref, t, me, peer
            self.send, self.recv = send, recv_

        def copy(self, n, arriving=False):
            step = (1, 1, 3, 3, 1, 3)[n]
            half = (0, 1, 1, 0, 0, 1)[n]
            slot = self.me if n < 4 else lax.rem(self.me + 4 - step, 4)
            target = slot
            if arriving:
                target = lax.rem(self.me + 4 - step, 4) if n < 4 else lax.rem(self.me + 2, 4)
            at = pl.ds(half * (B // 2), B // 2)
            return remote(
                self.ref.at[slot, self.t, at], self.ref.at[target, self.t, at],
                self.send.at[self.t, n], self.recv.at[self.t, n], (self.peer(step), e),
            )

        def start(self):
            for n in (0, 2, 1, 3):
                self.copy(n).start()

        def forward(self):
            self.copy(0, True).wait_recv()
            self.copy(4).start()
            self.copy(2, True).wait_recv()
            self.copy(5).start()

        def finish(self):
            for n in (1, 3, 4, 5):
                self.copy(n, True).wait_recv()

        def drain(self):
            for n in range(6):
                self.copy(n).wait_send()

    xo = Ring(xs, 0, x, xpeer, x_send, x_recv)
    xp = Ring(xs, 1, x, xpeer, x_send, x_recv)
    yo = Ring(ys, 0, y, ypeer, y_send, y_recv)
    yp = Ring(ys, 1, y, ypeer, y_send, y_recv)

    def prod(p1, p2):
        return mul(lhs(p1), rhs(p2))

    FOLD_CUT = 4
    lax.fori_loop(0, FOLD_CUT, fold, 0)
    pair(1).wait_recv()
    xs[x, 1] = prod(tbuf[0, 1], tbuf[1, 1])
    xp.start()
    lax.fori_loop(FOLD_CUT, S, fold, 0)
    pair(0).start()
    tbuf[core, 0] = own[core, 0]
    xp.forward()
    pair(0).wait_recv()
    xs[x, 0] = apply_map(tbuf[0, 0], tbuf[0, 1], tbuf[1, 0])
    xo.start()

    def prepare(i):
        flip(i)
        uh, ul = split(u[i])
        uu = jnp.concatenate([uh, ul], 1)
        for k in range(2):
            a0, ps = ap[k, 0], ap[k, 1]
            gi, gti = cat(g, i, k), gt[i, k]
            lg = lhs(gi)
            lt = lhs(gti)
            h0 = mul(lt, rhs(a0))
            w0[i, k] = mul(lhs(h0), rhs(gti))
            pw = rhs(ps)
            q[i, k] = lhs(mul(lt, pw))
            gg[i, k] = mul(lg, pw)
            rows = [gi[:, :B], -gi[:, B:], gti[:, :B], -gti[:, B:]]
            xh, xl = split(jnp.concatenate(rows, 0))
            t = dot(xh, uu)
            vh, vl = split(t[:, :B] + t[:, B:] + dot(xl, uh))
            for n in range(4):
                column = (n // 2) * 512 + k * 256 + (n % 2) * B
                vv[i, 0:B, column : column + B] = vh[n * B : n * B + B]
                vv[i, B : 2 * B, column : column + B] = vl[n * B : n * B + B]

    def step_back(i):
        for k in range(2):
            lk = link[i, k]
            left = lhs(lk)
            yk = mul(left, rhs(ap[k, 0]))
            pk = mul(left, rhs(ap[k, 1]))
            ap[k, 1] = pk
            ap[k, 0] = cat(c, i, k) + mul(lhs(yk), rhs_t(lk), True)

    zero = jnp.zeros((B, 2 * B), F32)
    for k in range(2):
        ap[k, 0] = cat(c, S - 1, k)
        ap[k, 1] = jnp.concatenate([last_u, jnp.zeros((B, B), F32)], 1)

    def level_p(ref, n):
        lp[n, 0] = prod(ref[0, 1], ref[1, 1])
        lp[n, 1] = prod(ref[2, 1], ref[3, 1])

    def level_o(ref, n):
        o01 = apply_map(ref[0, 0], ref[0, 1], ref[1, 0])
        o23 = apply_map(ref[2, 0], ref[2, 1], ref[3, 0])
        lo[n] = o23
        return apply_map(o01, lp[n, 0], o23)

    row_i = lax.broadcasted_iota(jnp.int32, (B, 2 * B), 0)
    col_i = lax.broadcasted_iota(jnp.int32, (B, 2 * B), 1)
    unit = jnp.where(row_i == col_i, 1.0, 0.0).astype(F32)

    def later(ref, out, n):
        o, p = combine((ref[1, 0], ref[1, 1]), (lo[n], lp[n, 1]))
        out[0, 0] = o
        out[0, 1] = p
        out[1, 0] = lo[n]
        out[1, 1] = lp[n, 1]
        out[2] = ref[3]
        out[3, 0] = zero
        out[3, 1] = unit

    zcopy = remote(zbuf, zrecv, z_sem.at[0], z_sem.at[1], (zpeer, e))

    def shadow(j, carry):
        i = S - 1 - j

        @pl.when(j > 0)
        def _():
            step_back(i)

        prepare(i)

        @pl.when(j == 0)
        def _():
            xp.finish()
            level_p(xs, 0)
            ys[y, 1] = prod(lp[0, 0], lp[0, 1])
            yp.start()

        @pl.when(j == 1)
        def _():
            xo.forward()

        @pl.when(j == 2)
        def _():
            yp.forward()

        @pl.when(j == 3)
        def _():
            xo.finish()
            ys[y, 0] = level_o(xs, 0)
            yo.start()
            yp.finish()
            level_p(ys, 1)

        @pl.when(j == 4)
        def _():
            yo.forward()
            later(xs, ex, 0)

        @pl.when(j == 6)
        def _():
            yo.finish()
            zbuf[...] = level_o(ys, 1)

            @pl.when(z == 1)
            def _():
                zcopy.start()
                zrecv[...] = zero

        return carry

    lax.fori_loop(0, S, shadow, 0)

    later(ys, ey, 1)
    outer = combine((ex[x, 0], ex[x, 1]), (ey[y, 0], ey[y, 1]))
    inner = combine((tbuf[1, 0], tbuf[1, 1]), outer)

    @pl.when(z == 0)
    def _():
        zcopy.wait_recv()

    top = zrecv[...]
    chip_in = apply_map(outer[0], outer[1], top)
    core_in = apply_map(inner[0], inner[1], top)
    is_first = core == 0
    dbuf[...] = jnp.where(is_first, chip_in, core_in)
    down = remote(dbuf, xin.at[core], d_sem.at[0], d_sem.at[1], (partner, e))
    down.start()
    xin[core] = jnp.where(is_first, core_in, chip_in)
    down.wait_recv()

    for k in range(2):
        high, low = rhs(xin[k])
        xt[k, 0] = high
        xt[k, 1] = low

    def weights(i):
        for k in range(2):
            zk = mul(q[i, k], (xt[k, 0], xt[k, 1]))
            w[i, k] = w0[i, k] + mul(lhs(zk), rhs_t(gg[i, k]), True)

    weights(0)
    halo = remote(w.at[0], w.at[S], h_sem.at[0], h_sem.at[1], (prev, e))
    halo.start()

    def spread(i, n):
        step = (3, 1, 1, 3)[n]
        kind = (0, 1, 0, 1)[n]
        owner = epeer(2) if n < 2 else epeer(step)
        target = relay.at[i, kind] if n < 2 else recv.at[i, 0, kind]
        return remote(
            part.at[i, owner, kind], target,
            r_send.at[i, n], r_recv.at[i, n], (s, epeer(step)),
        )

    def pass_on(i, kind):
        step = (3, 1)[kind]
        return remote(
            relay.at[i, kind], recv.at[i, 1, kind],
            r_send.at[i, 4 + kind], r_recv.at[i, 4 + kind], (s, epeer(step)),
        )

    def finals(i, carry):
        @pl.when(i < S - 1)
        def _():
            weights(i + 1)

        @pl.when(i == S - 1)
        def _():
            halo.wait_recv()

            @pl.when(last)
            def _():
                for k in range(2):
                    w[S, k] = zero

        wh0, wl0 = split(w[i + 1, 0])
        wh1, wl1 = split(w[i + 1, 1])
        nt = jnp.concatenate(
            [jnp.concatenate([wh0, wh1], 1), jnp.concatenate([wl0, wl1], 1)], 0
        )
        nn = jnp.concatenate(
            [
                jnp.concatenate([h[:, m : m + B], l[:, m : m + B]], 1)
                for h, l in ((wh0, wl0), (wh1, wl1))
                for m in (0, B)
            ],
            0,
        )
        t = dot(vv[i, :, 0:512], nt, True) + dot(vv[i, :, 512:1024], nn)
        coupling = t[:B, :B] + (t[:B, B:] + t[B:, :B])
        onsite = w[i, 0, :, 0:B] + w[i, 1, :, 0:B]
        for r in range(4):
            part[i, r, 0] = onsite[r * ROWS : (r + 1) * ROWS]
            part[i, r, 1] = coupling[r * ROWS : (r + 1) * ROWS]
        for n in range(4):
            spread(i, n).start()
        return carry

    lax.fori_loop(0, S, finals, 0)

    def pass_all(i, carry):
        for kind, step in ((0, 3), (1, 1)):
            spread(i, kind).wait_recv()
            relay[i, kind] += part[i, epeer(step), kind]
            pass_on(i, kind).start()
        return carry

    lax.fori_loop(0, S, pass_all, 0)

    def collect(i, carry):
        for kind, out in ((0, on_ref), (1, cp_ref)):
            spread(i, 2 + kind).wait_recv()
            pass_on(i, kind).wait_recv()
            out[i] = part[i, e, kind] + recv[i, 0, kind] + recv[i, 1, kind]
        return carry

    lax.fori_loop(0, S, collect, 0)

    for t in range(2):
        pair(t).wait_send()
    for ring in (xp, xo, yp, yo):
        ring.drain()

    @pl.when(z == 1)
    def _():
        zcopy.wait_send()

    down.wait_send()
    halo.wait_send()

    def drain(i, carry):
        for n in range(4):
            spread(i, n).wait_send()
        for kind in range(2):
            pass_on(i, kind).wait_send()
        return carry

    lax.fori_loop(0, S, drain, 0)


def on_device(green_blocks, couplings, green_cotangent):
    shape = (S, 2, 2, B, B)
    block = (B, 2 * B)
    vmem = pltpu.VMEM
    out = jax.ShapeDtypeStruct((S, ROWS, B), F32)
    dma = pltpu.SemaphoreType.DMA
    return pl.pallas_call(
        kernel,
        out_shape=(out, out),
        in_specs=[pl.BlockSpec(memory_space=pl.ANY)] * 3,
        out_specs=(pl.BlockSpec(memory_space=vmem),) * 2,
        scratch_shapes=[
            vmem(shape, F32),
            vmem((S, B, B), F32),
            vmem(shape, F32),
            vmem((S, 2) + block, F32),
            vmem((S, 2) + block, F32),
            vmem((2, 2) + block, F32),
            vmem((2, 2) + block, F32),
            vmem((NX, 2) + block, F32),
            vmem((NY, 2) + block, F32),
            vmem((NX, 2) + block, F32),
            vmem((NY, 2) + block, F32),
            vmem((2, 2) + block, F32),
            vmem((2,) + block, F32),
            vmem(block, F32),
            vmem(block, F32),
            vmem(block, F32),
            vmem((2,) + block, F32),
            vmem((2, 2) + block, F32),
            vmem((S, 2) + block, F32),
            vmem((S, 2) + block, F32),
            vmem((S, 2, 2 * B, 2 * B), BF16),
            vmem((S, 2) + block, F32),
            vmem((S, 2 * B, 8 * B), BF16),
            vmem((2, 2, 2 * B, 2 * B), BF16),
            vmem((S + 1, 2) + block, F32),
            vmem((S, 4, 2, ROWS, B), F32),
            vmem((S, 2, ROWS, B), F32),
            vmem((S, 2, 2, ROWS, B), F32),
            dma((S,)),
            dma((2,)),
            dma((2, 2)),
            dma((2, 6)),
            dma((2, 6)),
            dma((2, 6)),
            dma((2, 6)),
            dma((2,)),
            dma((2,)),
            dma((2,)),
            dma((S, 6)),
            dma((S, 6)),
        ],
        compiler_params=pltpu.CompilerParams(
            collective_id=0, has_side_effects=True, vmem_limit_bytes=62 * 1024 * 1024
        ),
    )(
        green_blocks.reshape(shape),
        couplings,
        green_cotangent.reshape(shape),
    )


def solution(mesh):
    in_specs = (
        P("slab", "energy", None, None, None, None),
        P("slab", None, None),
        P("slab", "energy", None, None, None, None),
    )
    out_specs = (P("slab", "energy", None), P("slab", "energy", None))
    return jax.shard_map(
        on_device, mesh=mesh, in_specs=in_specs, out_specs=out_specs, check_vma=False
    )
```

```python
import functools

import jax
import jax.numpy as jnp
from jax import lax
from jax.experimental import pallas as pl
from jax.experimental.pallas import tpu as pltpu
from jax.sharding import PartitionSpec as P

F32 = jnp.float32
BF16 = jnp.bfloat16
MESH = pl.DeviceIdType.MESH
B = 128
S = 8
ROWS = 32
NX, NY = 4, 4
EARLY = 3


def split(a):
    high = a.astype(BF16)
    return high, (a - high.astype(F32)).astype(BF16)


def dot(a, b, nt=False):
    return lax.dot_general(
        a, b, (((1,), (1 if nt else 0,)), ((), ())), preferred_element_type=F32
    )


def wide(b):
    re, im = b[:, :B], b[:, B:]
    return jnp.concatenate([b, jnp.concatenate([-im, re], 1)], 0)


def wide_t(b):
    re, im = b[:, :B], b[:, B:]
    return jnp.concatenate(
        [jnp.concatenate([re, -im], 1), jnp.concatenate([im, re], 1)], 0
    )


def lhs(x):
    high, low = split(x)
    return jnp.concatenate([high, low], 0)


def rhs(b):
    high, low = split(b)
    return wide(high), wide(low)


def rhs_t(b):
    high, low = split(b)
    return wide_t(high), wide_t(low)


def mul(x, w, nt=False):
    rows = x.shape[0] // 2
    y = dot(x, w[0], nt)
    return y[:rows] + y[rows:] + dot(x[:rows], w[1], nt)


def apply_map(off, prod, inner):
    return off + mul(lhs(mul(lhs(prod), rhs(inner))), rhs_t(prod), True)


def combine(first, second):
    off1, p1 = first
    off2, p2 = second
    left = lhs(p1)
    y = mul(left, rhs(off2))
    prod = mul(left, rhs(p2))
    return off1 + mul(lhs(y), rhs_t(p1), True), prod


def kernel(
    g_hbm, u_hbm, c_hbm, on_ref, cp_ref,
    g, u, c, link, pre, own, tbuf, xs, ys, ex, ey, lp, lo, zbuf, dbuf, zrecv, xin,
    ap, maps, w0, q, gg, vv, xt, w,
    stage, up, down_rows, mid, kept, from_below, from_above, passed,
    g_sem, in_sem, pair_sem, x_send, x_recv, y_send, y_recv, z_sem, d_sem, h_sem,
    r_send, r_recv, p_send, p_recv,
):
    s = lax.axis_index("slab")
    e = lax.axis_index("energy")
    core = lax.rem(s, 2)
    x = lax.rem(s // 2, NX)
    y = lax.rem(s // (2 * NX), NY)
    z = s // (2 * NX * NY)
    slabs = 2 * NX * NY * 2
    prev = lax.rem(s + slabs - 1, slabs)
    after = lax.rem(s + 1, slabs)
    partner = s + 1 - 2 * core
    zpeer = lax.rem(s + slabs // 2, slabs)
    last = s == slabs - 1

    def xpeer(d):
        return s + (lax.rem(x + d, NX) - x) * 2

    def ypeer(d):
        return s + (lax.rem(y + d, NY) - y) * (2 * NX)

    def epeer(d):
        return lax.rem(e + d, 4)

    barrier = pltpu.get_barrier_semaphore()
    greet = [(prev, e), (after, e), (partner, e), (zpeer, e)]
    greet += [(xpeer(d), e) for d in (1, 3)]
    greet += [(ypeer(d), e) for d in (1, 3)]
    greet += [(s, epeer(d)) for d in (1, 3)]
    for device in greet:
        pl.semaphore_signal(barrier, inc=1, device_id=device, device_id_type=MESH)

    def g_copy(i):
        return pltpu.make_async_copy(g_hbm.at[i], g.at[i], g_sem.at[i])

    cu = pltpu.make_async_copy(u_hbm, u, in_sem.at[0])
    cc = pltpu.make_async_copy(c_hbm, c, in_sem.at[1])
    g_copy(0).start()
    cu.start()
    for i in range(1, S):
        g_copy(i).start()
    cc.start()

    def remote(src, dst, send, recv_, device):
        return pltpu.make_async_remote_copy(
            src_ref=src, dst_ref=dst, send_sem=send, recv_sem=recv_,
            device_id=device, device_id_type=MESH,
        )

    def cat(ref, i, k):
        return jnp.concatenate([ref[i, k, 0], ref[i, k, 1]], 1)

    g_copy(0).wait()
    for k in range(2):
        pre[0, k] = jnp.concatenate([g[0, k, 0].T, g[0, k, 1].T], 1)
    cu.wait()

    def make_link(i):
        g_copy(i + 1).wait()
        uu = lhs(u[i])
        for k in range(2):
            gh, gl = split(jnp.concatenate([g[i + 1, k, 0], g[i + 1, k, 1]], 0))
            link[i, k] = mul(uu, (gh, gl), True)

    make_link(0)
    make_link(1)
    for i in range(S - 1):
        for k in range(2):
            pre[i + 1, k] = mul(lhs(pre[i, k]), rhs(link[i, k]))
        if i < S - 3:
            make_link(i + 2)
    last_u = u[S - 1] * jnp.where(last, 0.0, 1.0).astype(F32)
    uw = split(last_u)
    for k in range(2):
        value = pre[S - 1, k]
        t = mul(lhs(jnp.concatenate([value[:, :B], value[:, B:]], 0)), uw)
        own[k, 1] = jnp.concatenate([t[:B], t[B:]], 1)

    pl.semaphore_wait(barrier, len(greet))

    def pair(t):
        return remote(
            own.at[1 - core, t], tbuf.at[core, t],
            pair_sem.at[0, t], pair_sem.at[1, t], (partner, e),
        )

    pair(1).start()
    tbuf[core, 1] = own[core, 1]
    cc.wait()
    for k in range(2):
        own[k, 0] = jnp.zeros((B, 2 * B), F32)

    def fold(n, carry):
        for k in range(2):
            total = own[k, 0]
            for m in range(2):
                i = 2 * n + m
                pk = pre[i, k]
                yk = mul(lhs(pk), rhs(cat(c, i, k)))
                total += mul(lhs(yk), rhs_t(pk), True)
            own[k, 0] = total
        return carry

    class Ring:
        def __init__(self, ref, t, me, peer, send, recv_):
            self.ref, self.t, self.me, self.peer = ref, t, me, peer
            self.send, self.recv = send, recv_

        def copy(self, n, arriving=False):
            step = (1, 1, 3, 3, 1, 3)[n]
            half = (0, 1, 1, 0, 0, 1)[n]
            slot = self.me if n < 4 else lax.rem(self.me + 4 - step, 4)
            target = slot
            if arriving:
                target = lax.rem(self.me + 4 - step, 4) if n < 4 else lax.rem(self.me + 2, 4)
            at = pl.ds(half * (B // 2), B // 2)
            return remote(
                self.ref.at[slot, self.t, at], self.ref.at[target, self.t, at],
                self.send.at[self.t, n], self.recv.at[self.t, n], (self.peer(step), e),
            )

        def start(self):
            for n in (0, 2, 1, 3):
                self.copy(n).start()

        def forward(self):
            self.copy(0, True).wait_recv()
            self.copy(4).start()
            self.copy(2, True).wait_recv()
            self.copy(5).start()

        def finish(self):
            for n in (1, 3, 4, 5):
                self.copy(n, True).wait_recv()

        def drain(self):
            for n in range(6):
                self.copy(n).wait_send()

    xo = Ring(xs, 0, x, xpeer, x_send, x_recv)
    xp = Ring(xs, 1, x, xpeer, x_send, x_recv)
    yo = Ring(ys, 0, y, ypeer, y_send, y_recv)
    yp = Ring(ys, 1, y, ypeer, y_send, y_recv)

    def prod(p1, p2):
        return mul(lhs(p1), rhs(p2))

    lax.fori_loop(0, 1, fold, 0)
    pair(1).wait_recv()
    xs[x, 1] = prod(tbuf[0, 1], tbuf[1, 1])
    xp.start()

    lax.fori_loop(1, S // 2, fold, 0)
    pair(0).start()
    tbuf[core, 0] = own[core, 0]
    xp.forward()
    pair(0).wait_recv()
    xs[x, 0] = apply_map(tbuf[0, 0], tbuf[0, 1], tbuf[1, 0])
    xo.start()

    def prepare(i, k):
        uh, ul = split(u[i])
        uu = jnp.concatenate([uh, ul], 1)
        gi = cat(g, i, k)
        gti = jnp.concatenate([g[i, k, 0].T, g[i, k, 1].T], 1)
        lg = lhs(gi)
        lt = lhs(gti)
        h0 = mul(lt, rhs(ap[i, k, 0]))
        pw = rhs(ap[i, k, 1])
        q[i, k] = lhs(mul(lt, pw))
        gg[i, k] = mul(lg, pw)
        w0[i, k] = mul(lhs(h0), rhs(gti))
        rows = [gi[:, :B], -gi[:, B:], gti[:, :B], -gti[:, B:]]
        xh, xl = split(jnp.concatenate(rows, 0))
        t = dot(xh, uu)
        vh, vl = split(t[:, :B] + t[:, B:] + dot(xl, uh))
        for n in range(4):
            row = n * B
            column = (n % 2) * B
            vv[i, k, n // 2, 0:B, column : column + B] = vh[row : row + B]
            vv[i, k, n // 2, B : 2 * B, column : column + B] = vl[row : row + B]

    def step_back(i, k):
        lk = link[i, k]
        left = lhs(lk)
        yk = mul(left, rhs(ap[i + 1, k, 0]))
        ap[i, k, 1] = mul(left, rhs(ap[i + 1, k, 1]))
        ap[i, k, 0] = cat(c, i, k) + mul(lhs(yk), rhs_t(lk), True)

    zero = jnp.zeros((B, 2 * B), F32)
    for k in range(2):
        ap[S - 1, k, 0] = cat(c, S - 1, k)
        ap[S - 1, k, 1] = jnp.concatenate([last_u, jnp.zeros((B, B), F32)], 1)

    def level_p(ref, n):
        lp[n, 0] = prod(ref[0, 1], ref[1, 1])
        lp[n, 1] = prod(ref[2, 1], ref[3, 1])

    def level_o(ref, n):
        o01 = apply_map(ref[0, 0], ref[0, 1], ref[1, 0])
        o23 = apply_map(ref[2, 0], ref[2, 1], ref[3, 0])
        lo[n] = o23
        return apply_map(o01, lp[n, 0], o23)

    row_i = lax.broadcasted_iota(jnp.int32, (B, 2 * B), 0)
    col_i = lax.broadcasted_iota(jnp.int32, (B, 2 * B), 1)
    unit = jnp.where(row_i == col_i, 1.0, 0.0).astype(F32)

    def later(ref, out, n):
        o, p = combine((ref[1, 0], ref[1, 1]), (lo[n], lp[n, 1]))
        out[0, 0] = o
        out[0, 1] = p
        out[1, 0] = lo[n]
        out[1, 1] = lp[n, 1]
        out[2] = ref[3]
        out[3, 0] = zero
        out[3, 1] = unit

    zcopy = remote(zbuf, zrecv, z_sem.at[0], z_sem.at[1], (zpeer, e))

    def shadow(j, carry):
        i = S - 1 - j // 2
        k = lax.rem(j, 2)
        step_back(i, k)

        @pl.when(i < EARLY)
        def _():
            prepare(i, k)

        @pl.when(j == 4)
        def _():
            xp.finish()
            level_p(xs, 0)
            ys[y, 1] = prod(lp[0, 0], lp[0, 1])
            yp.start()

        @pl.when(j == 5)
        def _():
            xo.forward()

        @pl.when(j == 8)
        def _():
            yp.forward()

        @pl.when(j == 10)
        def _():
            xo.finish()
            ys[y, 0] = level_o(xs, 0)
            yo.start()
            yp.finish()
            level_p(ys, 1)

        @pl.when(j == 12)
        def _():
            yo.forward()
            later(xs, ex, 0)
            o, p = combine((tbuf[1, 0], tbuf[1, 1]), (ex[x, 0], ex[x, 1]))
            maps[0, 0] = ex[x, 0]
            maps[0, 1] = ex[x, 1]
            maps[1, 0] = o
            maps[1, 1] = p

        return carry

    lax.fori_loop(2, 2 * S, shadow, 0)
    yo.finish()
    zbuf[...] = level_o(ys, 1)

    @pl.when(z == 1)
    def _():
        zcopy.start()

    later(ys, ey, 1)
    outer_y = (ey[y, 0], ey[y, 1])
    for n in range(2):
        o, p = combine((maps[n, 0], maps[n, 1]), outer_y)
        maps[n, 0] = o
        maps[n, 1] = p

    give, keep = core, 1 - core

    @pl.when(z == 1)
    def _():
        dbuf[...] = maps[give, 0]
        xin[core] = maps[keep, 0]

    @pl.when(z == 0)
    def _():
        for k in range(2):
            prepare(EARLY, k)
        zcopy.wait_recv()
        dbuf[...] = apply_map(maps[give, 0], maps[give, 1], zrecv[...])

    down = remote(dbuf, xin.at[core], d_sem.at[0], d_sem.at[1], (partner, e))
    down.start()

    @pl.when(z == 0)
    def _():
        xin[core] = apply_map(maps[keep, 0], maps[keep, 1], zrecv[...])

    def weigh(i, k):
        zk = mul(q[i, k], (xt[k, 0], xt[k, 1]))
        w[i, k] = w0[i, k] + mul(lhs(zk), rhs_t(gg[i, k]), True)

    def first_weights(n, carry):
        k = jnp.where(n == 0, core, 1 - core)

        @pl.when(n == 1)
        def _():
            down.wait_recv()

        high, low = rhs(xin[k])
        xt[k, 0] = high
        xt[k, 1] = low
        weigh(0, k)
        return carry

    lax.fori_loop(0, 2, first_weights, 0)
    halo = remote(w.at[0], w.at[S], h_sem.at[0], h_sem.at[1], (prev, e))

    @pl.when(s > 0)
    def _():
        halo.start()

    ready = EARLY + 1 - z

    def spread(i, n):
        return remote(
            (up, down_rows)[n].at[i], (from_below, from_above)[n].at[i],
            r_send.at[i, n], r_recv.at[i, n], (s, epeer((1, 3)[n])),
        )

    def pass_on(pair_no, kind):
        at = pl.ds(2 * pair_no, 2)
        return remote(
            mid.at[kind, at], passed.at[kind, at],
            p_send.at[pair_no, kind], p_recv.at[pair_no, kind], (s, epeer((3, 1)[kind])),
        )

    def rows_of(kind, d):
        return stage[kind, pl.ds(pl.multiple_of(epeer(d) * ROWS, ROWS), ROWS)]

    def pass_step(pair_no, carry):
        for m in range(2):
            i = 2 * pair_no + m
            for n in range(2):
                spread(i, n).wait_recv()
            mid[0, i] += from_above[i, 0]
            mid[1, i] += from_below[i, 1]
        for kind in range(2):
            pass_on(pair_no, kind).start()
        return carry

    def finals(i, carry):
        stage[0] = w[i, 0, :, 0:B] + w[i, 1, :, 0:B]

        @pl.when((i < S - 1) & (i + 1 >= ready))
        def _():
            for k in range(2):
                prepare(i + 1, k)

        @pl.when(i < S - 1)
        def _():
            for k in range(2):
                weigh(i + 1, k)

        @pl.when(i == S - 1)
        def _():
            @pl.when(s < slabs - 1)
            def _():
                halo.wait_recv()

            @pl.when(last)
            def _():
                for k in range(2):
                    w[S, k] = zero

        t = None
        for k in range(2):
            wh, wl = split(w[i + 1, k])
            nt = jnp.concatenate([wh, wl], 0)
            nn = jnp.concatenate(
                [jnp.concatenate([wh[:, m : m + B], wl[:, m : m + B]], 1) for m in (0, B)], 0
            )
            tk = dot(vv[i, k, 0], nt, True) + dot(vv[i, k, 1], nn)
            t = tk if t is None else t + tk
        stage[1] = t[:B, :B] + (t[:B, B:] + t[B:, :B])
        up[i, 0] = rows_of(0, 1)
        up[i, 1] = rows_of(1, 2)
        down_rows[i, 0] = rows_of(0, 2)
        down_rows[i, 1] = rows_of(1, 3)
        for n in range(2):
            spread(i, n).start()
        mid[0, i] = rows_of(0, 3)
        mid[1, i] = rows_of(1, 1)
        for kind in range(2):
            kept[i, kind] = rows_of(kind, 0)
        return carry

    lax.fori_loop(0, S, finals, 0)
    lax.fori_loop(0, S // 2, pass_step, 0)

    def collect(pair_no, carry):
        for kind in range(2):
            pass_on(pair_no, kind).wait_recv()
        for m in range(2):
            i = 2 * pair_no + m
            on_ref[i] = kept[i, 0] + from_below[i, 0] + passed[0, i]
            cp_ref[i] = kept[i, 1] + from_above[i, 1] + passed[1, i]
        return carry

    lax.fori_loop(0, S // 2, collect, 0)

    for t in range(2):
        pair(t).wait_send()
    for ring in (xp, xo, yp, yo):
        ring.drain()

    @pl.when(z == 1)
    def _():
        zcopy.wait_send()

    down.wait_send()

    @pl.when(s > 0)
    def _():
        halo.wait_send()

    def drain(i, carry):
        for n in range(2):
            spread(2 * i, n).wait_send()
            spread(2 * i + 1, n).wait_send()
            pass_on(i, n).wait_send()
        return carry

    lax.fori_loop(0, S // 2, drain, 0)


def on_device(green_blocks, couplings, green_cotangent):
    shape = (S, 2, 2, B, B)
    block = (B, 2 * B)
    vmem = pltpu.VMEM
    out = jax.ShapeDtypeStruct((S, ROWS, B), F32)
    dma = pltpu.SemaphoreType.DMA
    return pl.pallas_call(
        kernel,
        out_shape=(out, out),
        in_specs=[pl.BlockSpec(memory_space=pl.ANY)] * 3,
        out_specs=(pl.BlockSpec(memory_space=vmem),) * 2,
        scratch_shapes=[
            vmem(shape, F32),
            vmem((S, B, B), F32),
            vmem(shape, F32),
            vmem((S, 2) + block, F32),
            vmem((S, 2) + block, F32),
            vmem((2, 2) + block, F32),
            vmem((2, 2) + block, F32),
            vmem((NX, 2) + block, F32),
            vmem((NY, 2) + block, F32),
            vmem((NX, 2) + block, F32),
            vmem((NY, 2) + block, F32),
            vmem((2, 2) + block, F32),
            vmem((2,) + block, F32),
            vmem(block, F32),
            vmem(block, F32),
            vmem(block, F32),
            vmem((2,) + block, F32),
            vmem((S, 2, 2) + block, F32),
            vmem((2, 2) + block, F32),
            vmem((S, 2) + block, F32),
            vmem((S, 2, 2 * B, 2 * B), BF16),
            vmem((S, 2) + block, F32),
            vmem((S, 2, 2, 2 * B, 2 * B), BF16),
            vmem((2, 2, 2 * B, 2 * B), BF16),
            vmem((S + 1, 2) + block, F32),
            vmem((2, B, B), F32),
            vmem((S, 2, ROWS, B), F32),
            vmem((S, 2, ROWS, B), F32),
            vmem((2, S, ROWS, B), F32),
            vmem((S, 2, ROWS, B), F32),
            vmem((S, 2, ROWS, B), F32),
            vmem((S, 2, ROWS, B), F32),
            vmem((2, S, ROWS, B), F32),
            dma((S,)),
            dma((2,)),
            dma((2, 2)),
            dma((2, 6)),
            dma((2, 6)),
            dma((2, 6)),
            dma((2, 6)),
            dma((2,)),
            dma((2,)),
            dma((2,)),
            dma((S, 2)),
            dma((S, 2)),
            dma((S // 2, 2)),
            dma((S // 2, 2)),
        ],
        compiler_params=pltpu.CompilerParams(
            collective_id=0, has_side_effects=True, vmem_limit_bytes=62 * 1024 * 1024
        ),
    )(
        green_blocks.reshape(shape),
        couplings,
        green_cotangent.reshape(shape),
    )


def solution(mesh):
    in_specs = (
        P("slab", "energy", None, None, None, None),
        P("slab", None, None),
        P("slab", "energy", None, None, None, None),
    )
    out_specs = (P("slab", "energy", None), P("slab", "energy", None))
    return jax.shard_map(
        on_device, mesh=mesh, in_specs=in_specs, out_specs=out_specs, check_vma=False
    )
```

```python
import functools

import jax
import jax.numpy as jnp
from jax import lax
from jax.experimental import pallas as pl
from jax.experimental.pallas import tpu as pltpu
from jax.sharding import PartitionSpec as P

F32 = jnp.float32
BF16 = jnp.bfloat16
MESH = pl.DeviceIdType.MESH
B = 128
S = 8
ROWS = 32
NX, NY = 4, 4
EARLY = 6


def split(a):
    high = a.astype(BF16)
    return high, (a - high.astype(F32)).astype(BF16)


def dot(a, b, nt=False):
    return lax.dot_general(
        a, b, (((1,), (1 if nt else 0,)), ((), ())), preferred_element_type=F32
    )


def wide(b):
    re, im = b[:, :B], b[:, B:]
    return jnp.concatenate([b, jnp.concatenate([-im, re], 1)], 0)


def wide_t(b):
    re, im = b[:, :B], b[:, B:]
    return jnp.concatenate(
        [jnp.concatenate([re, -im], 1), jnp.concatenate([im, re], 1)], 0
    )


def lhs(x):
    high, low = split(x)
    return jnp.concatenate([high, low], 0)


def rhs(b):
    high, low = split(b)
    return wide(high), wide(low)


def rhs_t(b):
    high, low = split(b)
    return wide_t(high), wide_t(low)


def mul(x, w, nt=False):
    rows = x.shape[0] // 2
    y = dot(x, w[0], nt)
    return y[:rows] + y[rows:] + dot(x[:rows], w[1], nt)


def apply_map(off, prod, inner):
    return off + mul(lhs(mul(lhs(prod), rhs(inner))), rhs_t(prod), True)


def combine(first, second):
    off1, p1 = first
    off2, p2 = second
    left = lhs(p1)
    y = mul(left, rhs(off2))
    prod = mul(left, rhs(p2))
    return off1 + mul(lhs(y), rhs_t(p1), True), prod


def kernel(
    g_hbm, u_hbm, c_hbm, on_ref, cp_ref,
    g, u, c, link, head, own, tbuf, xs, ys, ex, ey, lp, lo, zbuf, dbuf, zrecv, xin,
    ap, maps, w0, q, gg, vv, xt, w,
    stage, up, down_rows, mid, kept, from_below, from_above, passed,
    g_sem, in_sem, pair_sem, x_send, x_recv, y_send, y_recv, z_sem, d_sem, h_sem,
    r_send, r_recv, p_send, p_recv,
):
    s = lax.axis_index("slab")
    e = lax.axis_index("energy")
    core = lax.rem(s, 2)
    x = lax.rem(s // 2, NX)
    y = lax.rem(s // (2 * NX), NY)
    z = s // (2 * NX * NY)
    slabs = 2 * NX * NY * 2
    prev = lax.rem(s + slabs - 1, slabs)
    after = lax.rem(s + 1, slabs)
    partner = s + 1 - 2 * core
    zpeer = lax.rem(s + slabs // 2, slabs)
    last = s == slabs - 1

    def xpeer(d):
        return s + (lax.rem(x + d, NX) - x) * 2

    def ypeer(d):
        return s + (lax.rem(y + d, NY) - y) * (2 * NX)

    def epeer(d):
        return lax.rem(e + d, 4)

    barrier = pltpu.get_barrier_semaphore()
    greet = [(prev, e), (after, e), (partner, e), (zpeer, e)]
    greet += [(xpeer(d), e) for d in (1, 3)]
    greet += [(ypeer(d), e) for d in (1, 3)]
    greet += [(s, epeer(d)) for d in (1, 3)]
    for device in greet:
        pl.semaphore_signal(barrier, inc=1, device_id=device, device_id_type=MESH)

    def g_copy(i):
        return pltpu.make_async_copy(g_hbm.at[i], g.at[i], g_sem.at[i])

    cu = pltpu.make_async_copy(u_hbm, u, in_sem.at[0])
    cc = pltpu.make_async_copy(c_hbm, c, in_sem.at[1])
    g_copy(S - 1).start()
    cu.start()
    for i in range(S - 2, -1, -1):
        g_copy(i).start()
    cc.start()

    def remote(src, dst, send, recv_, device):
        return pltpu.make_async_remote_copy(
            src_ref=src, dst_ref=dst, send_sem=send, recv_sem=recv_,
            device_id=device, device_id_type=MESH,
        )

    def cat(ref, i, k):
        return jnp.concatenate([ref[i, k, 0], ref[i, k, 1]], 1)

    cu.wait()
    g_copy(S - 1).wait()
    last_u = u[S - 1] * jnp.where(last, 0.0, 1.0).astype(F32)
    for k in range(2):
        ap[S - 1, k, 1] = jnp.concatenate([last_u, jnp.zeros((B, B), F32)], 1)

    def make_link(i):
        uu = lhs(u[i])
        for k in range(2):
            gh, gl = split(jnp.concatenate([g[i + 1, k, 0], g[i + 1, k, 1]], 0))
            link[i, k] = mul(uu, (gh, gl), True)
        g_copy(i).wait()

    make_link(S - 2)
    make_link(S - 3)
    for i in range(S - 2, -1, -1):
        for k in range(2):
            ap[i, k, 1] = mul(lhs(link[i, k]), rhs(ap[i + 1, k, 1]))
        if i > 1:
            make_link(i - 2)
    for k in range(2):
        head[k] = jnp.concatenate([g[0, k, 0].T, g[0, k, 1].T], 1)
        own[k, 1] = mul(lhs(head[k]), rhs(ap[0, k, 1]))

    pl.semaphore_wait(barrier, len(greet))

    def pair(t):
        return remote(
            own.at[1 - core, t], tbuf.at[core, t],
            pair_sem.at[0, t], pair_sem.at[1, t], (partner, e),
        )

    pair(1).start()
    tbuf[core, 1] = own[core, 1]
    cc.wait()
    for k in range(2):
        ap[S - 1, k, 0] = cat(c, S - 1, k)

    def fold(i):
        lk = [link[i, k] for k in range(2)]
        half = [mul(lhs(lk[k]), rhs(ap[i + 1, k, 0])) for k in range(2)]
        for k in range(2):
            ap[i, k, 0] = cat(c, i, k) + mul(lhs(half[k]), rhs_t(lk[k]), True)

    class Ring:
        def __init__(self, ref, t, me, peer, send, recv_):
            self.ref, self.t, self.me, self.peer = ref, t, me, peer
            self.send, self.recv = send, recv_

        def copy(self, n, arriving=False):
            step = (1, 1, 3, 3, 1, 3)[n]
            half = (0, 1, 1, 0, 0, 1)[n]
            slot = self.me if n < 4 else lax.rem(self.me + 4 - step, 4)
            target = slot
            if arriving:
                target = lax.rem(self.me + 4 - step, 4) if n < 4 else lax.rem(self.me + 2, 4)
            at = pl.ds(half * (B // 2), B // 2)
            return remote(
                self.ref.at[slot, self.t, at], self.ref.at[target, self.t, at],
                self.send.at[self.t, n], self.recv.at[self.t, n], (self.peer(step), e),
            )

        def start(self):
            for n in (0, 2, 1, 3):
                self.copy(n).start()

        def forward(self):
            self.copy(0, True).wait_recv()
            self.copy(4).start()
            self.copy(2, True).wait_recv()
            self.copy(5).start()

        def finish(self):
            for n in (1, 3, 4, 5):
                self.copy(n, True).wait_recv()

        def drain(self):
            for n in range(6):
                self.copy(n).wait_send()

    xo = Ring(xs, 0, x, xpeer, x_send, x_recv)
    xp = Ring(xs, 1, x, xpeer, x_send, x_recv)
    yo = Ring(ys, 0, y, ypeer, y_send, y_recv)
    yp = Ring(ys, 1, y, ypeer, y_send, y_recv)

    def prod(p1, p2):
        return mul(lhs(p1), rhs(p2))

    for i in range(S - 2, S - 5, -1):
        fold(i)
    pair(1).wait_recv()
    xs[x, 1] = prod(tbuf[0, 1], tbuf[1, 1])
    xp.start()

    for i in range(S - 5, -1, -1):
        fold(i)
    half = [mul(lhs(head[k]), rhs(ap[0, k, 0])) for k in range(2)]
    for k in range(2):
        own[k, 0] = mul(lhs(half[k]), rhs_t(head[k]), True)
    pair(0).start()
    tbuf[core, 0] = own[core, 0]
    xp.forward()
    pair(0).wait_recv()
    xs[x, 0] = apply_map(tbuf[0, 0], tbuf[0, 1], tbuf[1, 0])
    xo.start()

    def prepare(i):
        uh, ul = split(u[i])
        uu = jnp.concatenate([uh, ul], 1)
        ks = range(2)
        gi = [cat(g, i, k) for k in ks]
        gti = [jnp.concatenate([g[i, k, 0].T, g[i, k, 1].T], 1) for k in ks]
        lt = [lhs(gti[k]) for k in ks]
        h0 = [mul(lt[k], rhs(ap[i, k, 0])) for k in ks]
        for k in ks:
            pw = rhs(ap[i, k, 1])
            q[i, k] = lhs(mul(lt[k], pw))
            gg[i, k] = mul(lhs(gi[k]), pw)
        for k in ks:
            w0[i, k] = mul(lhs(h0[k]), rhs(gti[k]))
        for k in ks:
            rows = [gi[k][:, :B], -gi[k][:, B:], gti[k][:, :B], -gti[k][:, B:]]
            xh, xl = split(jnp.concatenate(rows, 0))
            t = dot(xh, uu)
            vh, vl = split(t[:, :B] + t[:, B:] + dot(xl, uh))
            for n in range(4):
                row = n * B
                column = (n % 2) * B
                vv[i, n // 2, k, 0:B, column : column + B] = vh[row : row + B]
                vv[i, n // 2, k, B : 2 * B, column : column + B] = vl[row : row + B]

    zero = jnp.zeros((B, 2 * B), F32)

    def level_p(ref, n):
        lp[n, 0] = prod(ref[0, 1], ref[1, 1])
        lp[n, 1] = prod(ref[2, 1], ref[3, 1])

    def level_o(ref, n):
        half = [mul(lhs(ref[m, 1]), rhs(ref[m + 1, 0])) for m in (2, 0)]
        o23, o01 = [
            ref[m, 0] + mul(lhs(h), rhs_t(ref[m, 1]), True) for m, h in zip((2, 0), half)
        ]
        lo[n] = o23
        return apply_map(o01, lp[n, 0], o23)

    row_i = lax.broadcasted_iota(jnp.int32, (B, 2 * B), 0)
    col_i = lax.broadcasted_iota(jnp.int32, (B, 2 * B), 1)
    unit = jnp.where(row_i == col_i, 1.0, 0.0).astype(F32)

    def later(ref, out, n):
        o, p = combine((ref[1, 0], ref[1, 1]), (lo[n], lp[n, 1]))
        out[0, 0] = o
        out[0, 1] = p
        out[1, 0] = lo[n]
        out[1, 1] = lp[n, 1]
        out[2] = ref[3]
        out[3, 0] = zero
        out[3, 1] = unit

    zcopy = remote(zbuf, zrecv, z_sem.at[0], z_sem.at[1], (zpeer, e))

    prepare(0)
    xp.finish()
    level_p(xs, 0)
    ys[y, 1] = prod(lp[0, 0], lp[0, 1])
    yp.start()
    prepare(1)
    xo.forward()
    prepare(2)
    yp.forward()
    prepare(3)
    xo.finish()
    ys[y, 0] = level_o(xs, 0)
    yo.start()
    yp.finish()
    level_p(ys, 1)
    later(xs, ex, 0)
    o, p = combine((tbuf[1, 0], tbuf[1, 1]), (ex[x, 0], ex[x, 1]))
    maps[0, 0] = ex[x, 0]
    maps[0, 1] = ex[x, 1]
    maps[1, 0] = o
    maps[1, 1] = p
    yo.forward()
    for i in range(4, EARLY):
        prepare(i)
    yo.finish()
    zbuf[...] = level_o(ys, 1)

    @pl.when(z == 1)
    def _():
        zcopy.start()

    later(ys, ey, 1)
    outer_y = (ey[y, 0], ey[y, 1])
    ly = [lhs(maps[n, 1]) for n in range(2)]
    half = [mul(ly[n], rhs(ey[y, 0])) for n in range(2)]
    prods = [mul(ly[n], rhs(ey[y, 1])) for n in range(2)]
    offs = [
        maps[n, 0] + mul(lhs(half[n]), rhs_t(maps[n, 1]), True) for n in range(2)
    ]
    for n in range(2):
        maps[n, 0] = offs[n]
        maps[n, 1] = prods[n]

    give, keep = core, 1 - core

    @pl.when(z == 1)
    def _():
        dbuf[...] = maps[give, 0]
        xin[core] = maps[keep, 0]

    @pl.when(z == 0)
    def _():
        prepare(EARLY)
        zcopy.wait_recv()
        dbuf[...] = apply_map(maps[give, 0], maps[give, 1], zrecv[...])

    down = remote(dbuf, xin.at[core], d_sem.at[0], d_sem.at[1], (partner, e))
    down.start()

    @pl.when(z == 0)
    def _():
        xin[core] = apply_map(maps[keep, 0], maps[keep, 1], zrecv[...])

    def weigh(i, k):
        zk = mul(q[i, k], (xt[k, 0], xt[k, 1]))
        w[i, k] = w0[i, k] + mul(lhs(zk), rhs_t(gg[i, k]), True)

    def first_weights(n, carry):
        k = jnp.where(n == 0, core, 1 - core)

        @pl.when(n == 1)
        def _():
            down.wait_recv()

        high, low = rhs(xin[k])
        xt[k, 0] = high
        xt[k, 1] = low
        weigh(0, k)
        return carry

    lax.fori_loop(0, 2, first_weights, 0)
    halo = remote(w.at[0], w.at[S], h_sem.at[0], h_sem.at[1], (prev, e))

    @pl.when(s > 0)
    def _():
        halo.start()

    ready = EARLY + 1 - z

    def spread(i, n):
        return remote(
            (up, down_rows)[n].at[i], (from_below, from_above)[n].at[i],
            r_send.at[i, n], r_recv.at[i, n], (s, epeer((1, 3)[n])),
        )

    def pass_on(pair_no, kind):
        at = pl.ds(2 * pair_no, 2)
        return remote(
            mid.at[kind, at], passed.at[kind, at],
            p_send.at[pair_no, kind], p_recv.at[pair_no, kind], (s, epeer((3, 1)[kind])),
        )

    def rows_of(kind, d):
        return stage[kind, pl.ds(pl.multiple_of(epeer(d) * ROWS, ROWS), ROWS)]

    def pass_step(pair_no, carry):
        for m in range(2):
            i = 2 * pair_no + m
            for n in range(2):
                spread(i, n).wait_recv()
            mid[0, i] += from_above[i, 0]
            mid[1, i] += from_below[i, 1]
        for kind in range(2):
            pass_on(pair_no, kind).start()
        return carry

    def finals(i, carry):
        stage[0] = w[i, 0, :, 0:B] + w[i, 1, :, 0:B]

        @pl.when((i < S - 1) & (i + 1 >= ready))
        def _():
            prepare(i + 1)

        @pl.when(i < S - 1)
        def _():
            zs = [mul(q[i + 1, k], (xt[k, 0], xt[k, 1])) for k in range(2)]
            for k in range(2):
                w[i + 1, k] = w0[i + 1, k] + mul(lhs(zs[k]), rhs_t(gg[i + 1, k]), True)

        @pl.when(i == S - 1)
        def _():
            @pl.when(s < slabs - 1)
            def _():
                halo.wait_recv()

            @pl.when(last)
            def _():
                for k in range(2):
                    w[S, k] = zero

        nts, nns = [], []
        for k in range(2):
            wh, wl = split(w[i + 1, k])
            nts.append(jnp.concatenate([wh, wl], 0))
            for m in (0, B):
                nns.append(jnp.concatenate([wh[:, m : m + B], wl[:, m : m + B]], 1))
        t = dot(
            jnp.concatenate([vv[i, 0, 0], vv[i, 0, 1]], 1), jnp.concatenate(nts, 1), True
        ) + dot(jnp.concatenate([vv[i, 1, 0], vv[i, 1, 1]], 1), jnp.concatenate(nns, 0))
        stage[1] = t[:B, :B] + (t[:B, B:] + t[B:, :B])
        up[i, 0] = rows_of(0, 1)
        up[i, 1] = rows_of(1, 2)
        down_rows[i, 0] = rows_of(0, 2)
        down_rows[i, 1] = rows_of(1, 3)
        for n in range(2):
            spread(i, n).start()
        mid[0, i] = rows_of(0, 3)
        mid[1, i] = rows_of(1, 1)
        for kind in range(2):
            kept[i, kind] = rows_of(kind, 0)
        return carry

    lax.fori_loop(0, S, finals, 0)
    lax.fori_loop(0, S // 2, pass_step, 0)

    def collect(pair_no, carry):
        for kind in range(2):
            pass_on(pair_no, kind).wait_recv()
        for m in range(2):
            i = 2 * pair_no + m
            on_ref[i] = kept[i, 0] + from_below[i, 0] + passed[0, i]
            cp_ref[i] = kept[i, 1] + from_above[i, 1] + passed[1, i]
        return carry

    lax.fori_loop(0, S // 2, collect, 0)

    for t in range(2):
        pair(t).wait_send()
    for ring in (xp, xo, yp, yo):
        ring.drain()

    @pl.when(z == 1)
    def _():
        zcopy.wait_send()

    down.wait_send()

    @pl.when(s > 0)
    def _():
        halo.wait_send()

    def drain(i, carry):
        for n in range(2):
            spread(2 * i, n).wait_send()
            spread(2 * i + 1, n).wait_send()
            pass_on(i, n).wait_send()
        return carry

    lax.fori_loop(0, S // 2, drain, 0)


def on_device(green_blocks, couplings, green_cotangent):
    shape = (S, 2, 2, B, B)
    block = (B, 2 * B)
    vmem = pltpu.VMEM
    out = jax.ShapeDtypeStruct((S, ROWS, B), F32)
    dma = pltpu.SemaphoreType.DMA
    return pl.pallas_call(
        kernel,
        out_shape=(out, out),
        in_specs=[pl.BlockSpec(memory_space=pl.ANY)] * 3,
        out_specs=(pl.BlockSpec(memory_space=vmem),) * 2,
        scratch_shapes=[
            vmem(shape, F32),
            vmem((S, B, B), F32),
            vmem(shape, F32),
            vmem((S, 2) + block, F32),
            vmem((2,) + block, F32),
            vmem((2, 2) + block, F32),
            vmem((2, 2) + block, F32),
            vmem((NX, 2) + block, F32),
            vmem((NY, 2) + block, F32),
            vmem((NX, 2) + block, F32),
            vmem((NY, 2) + block, F32),
            vmem((2, 2) + block, F32),
            vmem((2,) + block, F32),
            vmem(block, F32),
            vmem(block, F32),
            vmem(block, F32),
            vmem((2,) + block, F32),
            vmem((S, 2, 2) + block, F32),
            vmem((2, 2) + block, F32),
            vmem((S, 2) + block, F32),
            vmem((S, 2, 2 * B, 2 * B), BF16),
            vmem((S, 2) + block, F32),
            vmem((S, 2, 2, 2 * B, 2 * B), BF16),
            vmem((2, 2, 2 * B, 2 * B), BF16),
            vmem((S + 1, 2) + block, F32),
            vmem((2, B, B), F32),
            vmem((S, 2, ROWS, B), F32),
            vmem((S, 2, ROWS, B), F32),
            vmem((2, S, ROWS, B), F32),
            vmem((S, 2, ROWS, B), F32),
            vmem((S, 2, ROWS, B), F32),
            vmem((S, 2, ROWS, B), F32),
            vmem((2, S, ROWS, B), F32),
            dma((S,)),
            dma((2,)),
            dma((2, 2)),
            dma((2, 6)),
            dma((2, 6)),
            dma((2, 6)),
            dma((2, 6)),
            dma((2,)),
            dma((2,)),
            dma((2,)),
            dma((S, 2)),
            dma((S, 2)),
            dma((S // 2, 2)),
            dma((S // 2, 2)),
        ],
        compiler_params=pltpu.CompilerParams(
            collective_id=0, has_side_effects=True, vmem_limit_bytes=62 * 1024 * 1024
        ),
    )(
        green_blocks.reshape(shape),
        couplings,
        green_cotangent.reshape(shape),
    )


def solution(mesh):
    in_specs = (
        P("slab", "energy", None, None, None, None),
        P("slab", None, None),
        P("slab", "energy", None, None, None, None),
    )
    out_specs = (P("slab", "energy", None), P("slab", "energy", None))
    return jax.shard_map(
        on_device, mesh=mesh, in_specs=in_specs, out_specs=out_specs, check_vma=False
    )
```

```python
import functools

import jax
import jax.numpy as jnp
from jax import lax
from jax.experimental import pallas as pl
from jax.experimental.pallas import tpu as pltpu
from jax.sharding import PartitionSpec as P

F32 = jnp.float32
BF16 = jnp.bfloat16
MESH = pl.DeviceIdType.MESH
B = 128
S = 8
ROWS = 32
NX, NY = 4, 4
RELAY_AT = (6, 7)
EARLY = 4


def split(a):
    high = a.astype(BF16)
    return high, (a - high.astype(F32)).astype(BF16)


def dot(a, b, nt=False):
    return lax.dot_general(
        a, b, (((1,), (1 if nt else 0,)), ((), ())), preferred_element_type=F32
    )


def wide(b):
    re, im = b[:, :B], b[:, B:]
    return jnp.concatenate([b, jnp.concatenate([-im, re], 1)], 0)


def wide_t(b):
    re, im = b[:, :B], b[:, B:]
    return jnp.concatenate(
        [jnp.concatenate([re, -im], 1), jnp.concatenate([im, re], 1)], 0
    )


def lhs(x):
    high, low = split(x)
    return jnp.concatenate([high, low], 0)


def rhs(b):
    high, low = split(b)
    return wide(high), wide(low)


def rhs_t(b):
    high, low = split(b)
    return wide_t(high), wide_t(low)


def mul(x, w, nt=False):
    rows = x.shape[0] // 2
    y = dot(x, w[0], nt)
    return y[:rows] + y[rows:] + dot(x[:rows], w[1], nt)


def apply_map(off, prod, inner):
    return off + mul(lhs(mul(lhs(prod), rhs(inner))), rhs_t(prod), True)


def combine(first, second):
    off1, p1 = first
    off2, p2 = second
    left = lhs(p1)
    y = mul(left, rhs(off2))
    prod = mul(left, rhs(p2))
    return off1 + mul(lhs(y), rhs_t(p1), True), prod


def kernel(
    g_hbm, u_hbm, c_hbm, on_ref, cp_ref,
    g, u, c, link, head, own, tbuf, xs, ys, ex, ey, lp, lo, zbuf, dbuf, zrecv, xin,
    ap, maps, mp, w0, q, gg, vv, xt, w,
    stage, up, down_rows, mid, kept, from_below, from_above, passed,
    g_sem, u_sem, in_sem, pair_sem, x_send, x_recv, y_send, y_recv, z_sem, d_sem, h_sem,
    r_send, r_recv, p_send, p_recv,
):
    s = lax.axis_index("slab")
    e = lax.axis_index("energy")
    core = lax.rem(s, 2)
    x = lax.rem(s // 2, NX)
    y = lax.rem(s // (2 * NX), NY)
    z = s // (2 * NX * NY)
    slabs = 2 * NX * NY * 2
    prev = lax.rem(s + slabs - 1, slabs)
    after = lax.rem(s + 1, slabs)
    partner = s + 1 - 2 * core
    zpeer = lax.rem(s + slabs // 2, slabs)
    last = s == slabs - 1

    def xpeer(d):
        return s + (lax.rem(x + d, NX) - x) * 2

    def ypeer(d):
        return s + (lax.rem(y + d, NY) - y) * (2 * NX)

    def epeer(d):
        return lax.rem(e + d, 4)

    barrier = pltpu.get_barrier_semaphore()
    greet = [(prev, e), (after, e), (partner, e), (zpeer, e)]
    greet += [(xpeer(d), e) for d in (1, 3)]
    greet += [(ypeer(d), e) for d in (1, 3)]
    greet += [(s, epeer(d)) for d in (1, 3)]
    for device in greet:
        pl.semaphore_signal(barrier, inc=1, device_id=device, device_id_type=MESH)

    def g_copy(i):
        return pltpu.make_async_copy(g_hbm.at[i], g.at[i], g_sem.at[i])

    def u_copy(i):
        return pltpu.make_async_copy(u_hbm.at[i], u.at[i], u_sem.at[i])

    cc = pltpu.make_async_copy(c_hbm, c, in_sem)
    for i in range(S - 1, -1, -1):
        u_copy(i).start()
        g_copy(i).start()
    cc.start()

    def remote(src, dst, send, recv_, device):
        return pltpu.make_async_remote_copy(
            src_ref=src, dst_ref=dst, send_sem=send, recv_sem=recv_,
            device_id=device, device_id_type=MESH,
        )

    def cat(ref, i, k):
        return jnp.concatenate([ref[i, k, 0], ref[i, k, 1]], 1)

    u_copy(S - 1).wait()
    last_u = u[S - 1] * jnp.where(last, 0.0, 1.0).astype(F32)
    for k in range(2):
        ap[S - 1, k, 1] = jnp.concatenate([last_u, jnp.zeros((B, B), F32)], 1)

    def make_link(i):
        u_copy(i).wait()
        g_copy(i + 1).wait()
        uu = lhs(u[i])
        for k in range(2):
            gh, gl = split(jnp.concatenate([g[i + 1, k, 0], g[i + 1, k, 1]], 0))
            link[i, k] = mul(uu, (gh, gl), True)

    make_link(S - 2)
    make_link(S - 3)
    for i in range(S - 2, -1, -1):
        for k in range(2):
            ap[i, k, 1] = mul(lhs(link[i, k]), rhs(ap[i + 1, k, 1]))
        if i > 1:
            make_link(i - 2)
    g_copy(0).wait()
    for k in range(2):
        head[k] = jnp.concatenate([g[0, k, 0].T, g[0, k, 1].T], 1)
        own[k, 1] = mul(lhs(head[k]), rhs(ap[0, k, 1]))

    pl.semaphore_wait(barrier, len(greet))

    def pair(t):
        return remote(
            own.at[1 - core, t], tbuf.at[core, t],
            pair_sem.at[0, t], pair_sem.at[1, t], (partner, e),
        )

    pair(1).start()
    tbuf[core, 1] = own[core, 1]
    cc.wait()
    for k in range(2):
        ap[S - 1, k, 0] = cat(c, S - 1, k)

    def fold(i):
        lk = [link[i, k] for k in range(2)]
        half = [mul(lhs(lk[k]), rhs(ap[i + 1, k, 0])) for k in range(2)]
        for k in range(2):
            ap[i, k, 0] = cat(c, i, k) + mul(lhs(half[k]), rhs_t(lk[k]), True)

    class Ring:
        def __init__(self, ref, t, me, peer, send, recv_):
            self.ref, self.t, self.me, self.peer = ref, t, me, peer
            self.send, self.recv = send, recv_

        def copy(self, n, arriving=False):
            step = (1, 1, 3, 3, 1, 3)[n]
            half = (0, 1, 1, 0, 0, 1)[n]
            slot = self.me if n < 4 else lax.rem(self.me + 4 - step, 4)
            target = slot
            if arriving:
                target = lax.rem(self.me + 4 - step, 4) if n < 4 else lax.rem(self.me + 2, 4)
            at = pl.ds(half * (B // 2), B // 2)
            return remote(
                self.ref.at[slot, self.t, at], self.ref.at[target, self.t, at],
                self.send.at[self.t, n], self.recv.at[self.t, n], (self.peer(step), e),
            )

        def start(self):
            for n in (0, 2, 1, 3):
                self.copy(n).start()

        def forward(self):
            self.copy(0, True).wait_recv()
            self.copy(4).start()
            self.copy(2, True).wait_recv()
            self.copy(5).start()

        def finish(self):
            for n in (1, 3, 4, 5):
                self.copy(n, True).wait_recv()

        def drain(self):
            for n in range(6):
                self.copy(n).wait_send()

    xo = Ring(xs, 0, x, xpeer, x_send, x_recv)
    xp = Ring(xs, 1, x, xpeer, x_send, x_recv)
    yo = Ring(ys, 0, y, ypeer, y_send, y_recv)
    yp = Ring(ys, 1, y, ypeer, y_send, y_recv)

    def prod(p1, p2):
        return mul(lhs(p1), rhs(p2))

    for i in range(S - 2, S - 5, -1):
        fold(i)
    pair(1).wait_recv()
    xs[x, 1] = prod(tbuf[0, 1], tbuf[1, 1])
    xp.start()

    for i in range(S - 5, -1, -1):
        fold(i)
    half = [mul(lhs(head[k]), rhs(ap[0, k, 0])) for k in range(2)]
    for k in range(2):
        own[k, 0] = mul(lhs(half[k]), rhs_t(head[k]), True)
    pair(0).start()
    tbuf[core, 0] = own[core, 0]
    xp.forward()
    pair(0).wait_recv()
    xs[x, 0] = apply_map(tbuf[0, 0], tbuf[0, 1], tbuf[1, 0])
    xo.start()

    def prepare(i):
        uh, ul = split(u[i])
        uu = jnp.concatenate([uh, ul], 1)
        ks = range(2)
        gi = [cat(g, i, k) for k in ks]
        gti = [jnp.concatenate([g[i, k, 0].T, g[i, k, 1].T], 1) for k in ks]
        lt = [lhs(gti[k]) for k in ks]
        h0 = [mul(lt[k], rhs(ap[i, k, 0])) for k in ks]
        for k in ks:
            pw = rhs(ap[i, k, 1])
            q[i, k] = lhs(mul(lt[k], pw))
            gg[i, k] = mul(lhs(gi[k]), pw)
        for k in ks:
            w0[i, k] = mul(lhs(h0[k]), rhs(gti[k]))
        for k in ks:
            rows = [gi[k][:, :B], -gi[k][:, B:], gti[k][:, :B], -gti[k][:, B:]]
            xh, xl = split(jnp.concatenate(rows, 0))
            t = dot(xh, uu)
            vh, vl = split(t[:, :B] + t[:, B:] + dot(xl, uh))
            for n in range(4):
                row = n * B
                column = (n % 2) * B
                vv[i, n // 2, k, 0:B, column : column + B] = vh[row : row + B]
                vv[i, n // 2, k, B : 2 * B, column : column + B] = vl[row : row + B]

    zero = jnp.zeros((B, 2 * B), F32)

    def level_p(ref, n):
        lp[n, 0] = prod(ref[0, 1], ref[1, 1])
        lp[n, 1] = prod(ref[2, 1], ref[3, 1])

    def level_o(ref, n):
        half = [mul(lhs(ref[m, 1]), rhs(ref[m + 1, 0])) for m in (2, 0)]
        o23, o01 = [
            ref[m, 0] + mul(lhs(h), rhs_t(ref[m, 1]), True) for m, h in zip((2, 0), half)
        ]
        lo[n] = o23
        return apply_map(o01, lp[n, 0], o23)

    row_i = lax.broadcasted_iota(jnp.int32, (B, 2 * B), 0)
    col_i = lax.broadcasted_iota(jnp.int32, (B, 2 * B), 1)
    unit = jnp.where(row_i == col_i, 1.0, 0.0).astype(F32)

    def later(ref, out, n):
        o, p = combine((ref[1, 0], ref[1, 1]), (lo[n], lp[n, 1]))
        out[0, 0] = o
        out[0, 1] = p
        out[1, 0] = lo[n]
        out[1, 1] = lp[n, 1]
        out[2] = ref[3]
        out[3, 0] = zero
        out[3, 1] = unit

    zcopy = remote(zbuf, zrecv, z_sem.at[0], z_sem.at[1], (zpeer, e))

    prepare(0)
    xp.finish()
    level_p(xs, 0)
    ys[y, 1] = prod(lp[0, 0], lp[0, 1])
    yp.start()
    prepare(1)
    xo.forward()
    prepare(2)
    yp.forward()
    prepare(3)
    xo.finish()
    ys[y, 0] = level_o(xs, 0)
    yo.start()
    yp.finish()
    level_p(ys, 1)
    later(xs, ex, 0)
    o, p = combine((tbuf[1, 0], tbuf[1, 1]), (ex[x, 0], ex[x, 1]))
    maps[0, 0] = ex[x, 0]
    maps[0, 1] = ex[x, 1]
    maps[1, 0] = o
    maps[1, 1] = p
    yo.forward()
    ey[0, 1] = prod(ys[1, 1], lp[1, 1])
    ey[1, 1] = lp[1, 1]
    ey[2, 1] = ys[3, 1]
    ey[3, 1] = unit
    ly = [lhs(maps[n, 1]) for n in range(2)]
    ry = rhs(ey[y, 1])
    for n in range(2):
        mp[n] = mul(ly[n], ry)
    for i in range(4, EARLY):
        prepare(i)
    yo.finish()
    zbuf[...] = level_o(ys, 1)

    @pl.when(z == 1)
    def _():
        zcopy.start()

    ey[0, 0] = apply_map(ys[1, 0], ys[1, 1], lo[1])
    ey[1, 0] = lo[1]
    ey[2, 0] = ys[3, 0]
    ey[3, 0] = zero
    ry = rhs(ey[y, 0])
    half = [mul(lhs(maps[n, 1]), ry) for n in range(2)]
    for n in range(2):
        maps[n, 0] += mul(lhs(half[n]), rhs_t(maps[n, 1]), True)

    give, keep = core, 1 - core

    @pl.when(z == 1)
    def _():
        dbuf[...] = maps[give, 0]
        xin[core] = maps[keep, 0]

    @pl.when(z == 0)
    def _():
        prepare(EARLY)
        zcopy.wait_recv()
        dbuf[...] = apply_map(maps[give, 0], mp[give], zrecv[...])

    down = remote(dbuf, xin.at[core], d_sem.at[0], d_sem.at[1], (partner, e))
    down.start()

    @pl.when(z == 0)
    def _():
        xin[core] = apply_map(maps[keep, 0], mp[keep], zrecv[...])

    def weigh(i, k):
        zk = mul(q[i, k], (xt[k, 0], xt[k, 1]))
        w[i, k] = w0[i, k] + mul(lhs(zk), rhs_t(gg[i, k]), True)

    def first_weights(n, carry):
        k = jnp.where(n == 0, core, 1 - core)

        @pl.when(n == 1)
        def _():
            down.wait_recv()

        high, low = rhs(xin[k])
        xt[k, 0] = high
        xt[k, 1] = low
        weigh(0, k)
        return carry

    lax.fori_loop(0, 2, first_weights, 0)
    halo = remote(w.at[0], w.at[S], h_sem.at[0], h_sem.at[1], (prev, e))

    @pl.when(s > 0)
    def _():
        halo.start()


    def spread(i, n):
        return remote(
            (up, down_rows)[n].at[i], (from_below, from_above)[n].at[i],
            r_send.at[i, n], r_recv.at[i, n], (s, epeer((1, 3)[n])),
        )

    def pass_on(pair_no, kind):
        at = pl.ds(2 * pair_no, 2)
        return remote(
            mid.at[kind, at], passed.at[kind, at],
            p_send.at[pair_no, kind], p_recv.at[pair_no, kind], (s, epeer((3, 1)[kind])),
        )

    def rows_of(kind, d):
        return stage[kind, pl.ds(pl.multiple_of(epeer(d) * ROWS, ROWS), ROWS)]

    def pass_step(pair_no, carry):
        for m in range(2):
            i = 2 * pair_no + m
            for n in range(2):
                spread(i, n).wait_recv()
            mid[0, i] += from_above[i, 0]
            mid[1, i] += from_below[i, 1]
        for kind in range(2):
            pass_on(pair_no, kind).start()
        return carry

    def finals(i):
        stage[0] = w[i, 0, :, 0:B] + w[i, 1, :, 0:B]
        if i + 1 == EARLY:

            @pl.when(z == 1)
            def _():
                prepare(EARLY)

        elif EARLY < i + 1 < S:
            prepare(i + 1)
        if i < S - 1:
            zs = [mul(q[i + 1, k], (xt[k, 0], xt[k, 1])) for k in range(2)]
            for k in range(2):
                w[i + 1, k] = w0[i + 1, k] + mul(lhs(zs[k]), rhs_t(gg[i + 1, k]), True)
        else:

            @pl.when(s < slabs - 1)
            def _():
                halo.wait_recv()

            @pl.when(last)
            def _():
                for k in range(2):
                    w[S, k] = zero

        nts, nns = [], []
        for k in range(2):
            wh, wl = split(w[i + 1, k])
            nts.append(jnp.concatenate([wh, wl], 0))
            for m in (0, B):
                nns.append(jnp.concatenate([wh[:, m : m + B], wl[:, m : m + B]], 1))
        t = dot(
            jnp.concatenate([vv[i, 0, 0], vv[i, 0, 1]], 1), jnp.concatenate(nts, 1), True
        ) + dot(jnp.concatenate([vv[i, 1, 0], vv[i, 1, 1]], 1), jnp.concatenate(nns, 0))
        stage[1] = t[:B, :B] + (t[:B, B:] + t[B:, :B])
        up[i, 0] = rows_of(0, 1)
        up[i, 1] = rows_of(1, 2)
        down_rows[i, 0] = rows_of(0, 2)
        down_rows[i, 1] = rows_of(1, 3)
        for n in range(2):
            spread(i, n).start()
        mid[0, i] = rows_of(0, 3)
        mid[1, i] = rows_of(1, 1)
        for kind in range(2):
            kept[i, kind] = rows_of(kind, 0)

    for i in range(S):
        finals(i)
        if i in RELAY_AT:
            pass_step(RELAY_AT.index(i), 0)
    lax.fori_loop(len(RELAY_AT), S // 2, pass_step, 0)

    def collect(pair_no, carry):
        for kind in range(2):
            pass_on(pair_no, kind).wait_recv()
        for m in range(2):
            i = 2 * pair_no + m
            on_ref[i] = kept[i, 0] + from_below[i, 0] + passed[0, i]
            cp_ref[i] = kept[i, 1] + from_above[i, 1] + passed[1, i]
        return carry

    lax.fori_loop(0, S // 2, collect, 0)

    for t in range(2):
        pair(t).wait_send()
    for ring in (xp, xo, yp, yo):
        ring.drain()

    @pl.when(z == 1)
    def _():
        zcopy.wait_send()

    down.wait_send()

    @pl.when(s > 0)
    def _():
        halo.wait_send()

    def drain(i, carry):
        for n in range(2):
            spread(2 * i, n).wait_send()
            spread(2 * i + 1, n).wait_send()
            pass_on(i, n).wait_send()
        return carry

    lax.fori_loop(0, S // 2, drain, 0)


def on_device(green_blocks, couplings, green_cotangent):
    shape = (S, 2, 2, B, B)
    block = (B, 2 * B)
    vmem = pltpu.VMEM
    out = jax.ShapeDtypeStruct((S, ROWS, B), F32)
    dma = pltpu.SemaphoreType.DMA
    return pl.pallas_call(
        kernel,
        out_shape=(out, out),
        in_specs=[pl.BlockSpec(memory_space=pl.ANY)] * 3,
        out_specs=(pl.BlockSpec(memory_space=vmem),) * 2,
        scratch_shapes=[
            vmem(shape, F32),
            vmem((S, B, B), F32),
            vmem(shape, F32),
            vmem((S, 2) + block, F32),
            vmem((2,) + block, F32),
            vmem((2, 2) + block, F32),
            vmem((2, 2) + block, F32),
            vmem((NX, 2) + block, F32),
            vmem((NY, 2) + block, F32),
            vmem((NX, 2) + block, F32),
            vmem((NY, 2) + block, F32),
            vmem((2, 2) + block, F32),
            vmem((2,) + block, F32),
            vmem(block, F32),
            vmem(block, F32),
            vmem(block, F32),
            vmem((2,) + block, F32),
            vmem((S, 2, 2) + block, F32),
            vmem((2, 2) + block, F32),
            vmem((2,) + block, F32),
            vmem((S, 2) + block, F32),
            vmem((S, 2, 2 * B, 2 * B), BF16),
            vmem((S, 2) + block, F32),
            vmem((S, 2, 2, 2 * B, 2 * B), BF16),
            vmem((2, 2, 2 * B, 2 * B), BF16),
            vmem((S + 1, 2) + block, F32),
            vmem((2, B, B), F32),
            vmem((S, 2, ROWS, B), F32),
            vmem((S, 2, ROWS, B), F32),
            vmem((2, S, ROWS, B), F32),
            vmem((S, 2, ROWS, B), F32),
            vmem((S, 2, ROWS, B), F32),
            vmem((S, 2, ROWS, B), F32),
            vmem((2, S, ROWS, B), F32),
            dma((S,)),
            dma((S,)),
            dma,
            dma((2, 2)),
            dma((2, 6)),
            dma((2, 6)),
            dma((2, 6)),
            dma((2, 6)),
            dma((2,)),
            dma((2,)),
            dma((2,)),
            dma((S, 2)),
            dma((S, 2)),
            dma((S // 2, 2)),
            dma((S // 2, 2)),
        ],
        compiler_params=pltpu.CompilerParams(
            collective_id=0, has_side_effects=True, vmem_limit_bytes=62 * 1024 * 1024
        ),
    )(
        green_blocks.reshape(shape),
        couplings,
        green_cotangent.reshape(shape),
    )


def solution(mesh):
    in_specs = (
        P("slab", "energy", None, None, None, None),
        P("slab", None, None),
        P("slab", "energy", None, None, None, None),
    )
    out_specs = (P("slab", "energy", None), P("slab", "energy", None))
    return jax.shard_map(
        on_device, mesh=mesh, in_specs=in_specs, out_specs=out_specs, check_vma=False
    )
```

```python
import functools

import jax
import jax.numpy as jnp
from jax import lax
from jax.experimental import pallas as pl
from jax.experimental.pallas import tpu as pltpu
from jax.sharding import PartitionSpec as P

F32 = jnp.float32
BF16 = jnp.bfloat16
MESH = pl.DeviceIdType.MESH
B = 128
S = 8
ROWS = 32
NX, NY = 4, 4
RELAY_AT = (6, 7)
EARLY = 5


def split(a):
    high = a.astype(BF16)
    return high, (a - high.astype(F32)).astype(BF16)


def dot(a, b, nt=False):
    return lax.dot_general(
        a, b, (((1,), (1 if nt else 0,)), ((), ())), preferred_element_type=F32
    )


def wide(b):
    re, im = b[:, :B], b[:, B:]
    return jnp.concatenate([b, jnp.concatenate([-im, re], 1)], 0)


def wide_t(b):
    re, im = b[:, :B], b[:, B:]
    return jnp.concatenate(
        [jnp.concatenate([re, -im], 1), jnp.concatenate([im, re], 1)], 0
    )


def lhs(x):
    high, low = split(x)
    return jnp.concatenate([high, low], 0)


def rhs(b):
    high, low = split(b)
    return wide(high), wide(low)


def rhs_t(b):
    high, low = split(b)
    return wide_t(high), wide_t(low)


def mul(x, w, nt=False):
    rows = x.shape[0] // 2
    y = dot(x, w[0], nt)
    return y[:rows] + y[rows:] + dot(x[:rows], w[1], nt)


def apply_map(off, prod, inner):
    return off + mul(lhs(mul(lhs(prod), rhs(inner))), rhs_t(prod), True)


def combine(first, second):
    off1, p1 = first
    off2, p2 = second
    left = lhs(p1)
    y = mul(left, rhs(off2))
    prod = mul(left, rhs(p2))
    return off1 + mul(lhs(y), rhs_t(p1), True), prod


def kernel(
    g_hbm, u_hbm, c_hbm, on_ref, cp_ref,
    g, u, c, link, head, own, tbuf, xs, ys, ex, ey, lp, lo, zbuf, dbuf, zrecv, xin,
    ap, maps, mp, w0, q, gg, vv, xt, w,
    stage, up, down_rows, mid, kept, from_below, from_above, passed,
    g_sem, u_sem, in_sem, pair_sem, x_send, x_recv, y_send, y_recv, z_sem, d_sem, h_sem,
    r_send, r_recv, p_send, p_recv,
):
    s = lax.axis_index("slab")
    e = lax.axis_index("energy")
    core = lax.rem(s, 2)
    x = lax.rem(s // 2, NX)
    y = lax.rem(s // (2 * NX), NY)
    z = s // (2 * NX * NY)
    slabs = 2 * NX * NY * 2
    prev = lax.rem(s + slabs - 1, slabs)
    after = lax.rem(s + 1, slabs)
    partner = s + 1 - 2 * core
    zpeer = lax.rem(s + slabs // 2, slabs)
    last = s == slabs - 1

    def xpeer(d):
        return s + (lax.rem(x + d, NX) - x) * 2

    def ypeer(d):
        return s + (lax.rem(y + d, NY) - y) * (2 * NX)

    def epeer(d):
        return lax.rem(e + d, 4)

    barrier = pltpu.get_barrier_semaphore()
    greet = [(prev, e), (after, e), (partner, e), (zpeer, e)]
    greet += [(xpeer(d), e) for d in (1, 3)]
    greet += [(ypeer(d), e) for d in (1, 3)]
    greet += [(s, epeer(d)) for d in (1, 3)]
    for device in greet:
        pl.semaphore_signal(barrier, inc=1, device_id=device, device_id_type=MESH)

    def g_copy(i):
        return pltpu.make_async_copy(g_hbm.at[i], g.at[i], g_sem.at[i])

    def u_copy(i):
        return pltpu.make_async_copy(u_hbm.at[i], u.at[i], u_sem.at[i])

    cc = pltpu.make_async_copy(c_hbm, c, in_sem)
    for i in range(S - 1, -1, -1):
        u_copy(i).start()
        g_copy(i).start()
    cc.start()

    def remote(src, dst, send, recv_, device):
        return pltpu.make_async_remote_copy(
            src_ref=src, dst_ref=dst, send_sem=send, recv_sem=recv_,
            device_id=device, device_id_type=MESH,
        )

    def cat(ref, i, k):
        return jnp.concatenate([ref[i, k, 0], ref[i, k, 1]], 1)

    u_copy(S - 1).wait()
    last_u = u[S - 1] * jnp.where(last, 0.0, 1.0).astype(F32)
    for k in range(2):
        ap[S - 1, k, 1] = jnp.concatenate([last_u, jnp.zeros((B, B), F32)], 1)

    def make_link(i):
        u_copy(i).wait()
        g_copy(i + 1).wait()
        uu = lhs(u[i])
        for k in range(2):
            gh, gl = split(jnp.concatenate([g[i + 1, k, 0], g[i + 1, k, 1]], 0))
            link[i, k] = mul(uu, (gh, gl), True)

    make_link(S - 2)
    make_link(S - 3)
    for i in range(S - 2, -1, -1):
        for k in range(2):
            ap[i, k, 1] = mul(lhs(link[i, k]), rhs(ap[i + 1, k, 1]))
        if i > 1:
            make_link(i - 2)
    g_copy(0).wait()
    for k in range(2):
        head[k] = jnp.concatenate([g[0, k, 0].T, g[0, k, 1].T], 1)
        own[k, 1] = mul(lhs(head[k]), rhs(ap[0, k, 1]))

    pl.semaphore_wait(barrier, len(greet))

    def pair(t):
        return remote(
            own.at[1 - core, t], tbuf.at[core, t],
            pair_sem.at[0, t], pair_sem.at[1, t], (partner, e),
        )

    pair(1).start()
    tbuf[core, 1] = own[core, 1]
    cc.wait()
    for k in range(2):
        ap[S - 1, k, 0] = cat(c, S - 1, k)

    def fold(i):
        lk = [link[i, k] for k in range(2)]
        half = [mul(lhs(lk[k]), rhs(ap[i + 1, k, 0])) for k in range(2)]
        for k in range(2):
            ap[i, k, 0] = cat(c, i, k) + mul(lhs(half[k]), rhs_t(lk[k]), True)

    class Ring:
        def __init__(self, ref, t, me, peer, send, recv_):
            self.ref, self.t, self.me, self.peer = ref, t, me, peer
            self.send, self.recv = send, recv_

        def copy(self, n, arriving=False):
            step = (1, 1, 3, 3, 1, 3)[n]
            half = (0, 1, 1, 0, 0, 1)[n]
            slot = self.me if n < 4 else lax.rem(self.me + 4 - step, 4)
            target = slot
            if arriving:
                target = lax.rem(self.me + 4 - step, 4) if n < 4 else lax.rem(self.me + 2, 4)
            at = pl.ds(half * (B // 2), B // 2)
            return remote(
                self.ref.at[slot, self.t, at], self.ref.at[target, self.t, at],
                self.send.at[self.t, n], self.recv.at[self.t, n], (self.peer(step), e),
            )

        def start(self):
            for n in (0, 2, 1, 3):
                self.copy(n).start()

        def forward(self):
            self.copy(0, True).wait_recv()
            self.copy(4).start()
            self.copy(2, True).wait_recv()
            self.copy(5).start()

        def finish(self):
            for n in (1, 3, 4, 5):
                self.copy(n, True).wait_recv()

        def drain(self):
            for n in range(6):
                self.copy(n).wait_send()

    xo = Ring(xs, 0, x, xpeer, x_send, x_recv)
    xp = Ring(xs, 1, x, xpeer, x_send, x_recv)
    yo = Ring(ys, 0, y, ypeer, y_send, y_recv)
    yp = Ring(ys, 1, y, ypeer, y_send, y_recv)

    def prod(p1, p2):
        return mul(lhs(p1), rhs(p2))

    for i in range(S - 2, S - 5, -1):
        fold(i)
    pair(1).wait_recv()
    xs[x, 1] = prod(tbuf[0, 1], tbuf[1, 1])
    xp.start()

    for i in range(S - 5, -1, -1):
        fold(i)
    half = [mul(lhs(head[k]), rhs(ap[0, k, 0])) for k in range(2)]
    for k in range(2):
        own[k, 0] = mul(lhs(half[k]), rhs_t(head[k]), True)
    pair(0).start()
    tbuf[core, 0] = own[core, 0]
    xp.forward()
    pair(0).wait_recv()
    xs[x, 0] = apply_map(tbuf[0, 0], tbuf[0, 1], tbuf[1, 0])
    xo.start()

    def prepare(i):
        uh, ul = split(u[i])
        uu = jnp.concatenate([uh, ul], 1)
        ks = range(2)
        gi = [cat(g, i, k) for k in ks]
        gti = [jnp.concatenate([g[i, k, 0].T, g[i, k, 1].T], 1) for k in ks]
        lt = [lhs(gti[k]) for k in ks]
        h0 = [mul(lt[k], rhs(ap[i, k, 0])) for k in ks]
        for k in ks:
            pw = rhs(ap[i, k, 1])
            q[i, k] = lhs(mul(lt[k], pw))
            gg[i, k] = mul(lhs(gi[k]), pw)
        for k in ks:
            w0[i, k] = mul(lhs(h0[k]), rhs(gti[k]))
        for k in ks:
            rows = [gi[k][:, :B], -gi[k][:, B:], gti[k][:, :B], -gti[k][:, B:]]
            xh, xl = split(jnp.concatenate(rows, 0))
            t = dot(xh, uu)
            vh, vl = split(t[:, :B] + t[:, B:] + dot(xl, uh))
            for n in range(4):
                row = n * B
                column = (n % 2) * B
                vv[i, n // 2, k, 0:B, column : column + B] = vh[row : row + B]
                vv[i, n // 2, k, B : 2 * B, column : column + B] = vl[row : row + B]

    zero = jnp.zeros((B, 2 * B), F32)

    def level_p(ref, n):
        lp[n, 0] = prod(ref[0, 1], ref[1, 1])
        lp[n, 1] = prod(ref[2, 1], ref[3, 1])

    def level_o(ref, n):
        half = [mul(lhs(ref[m, 1]), rhs(ref[m + 1, 0])) for m in (2, 0)]
        o23, o01 = [
            ref[m, 0] + mul(lhs(h), rhs_t(ref[m, 1]), True) for m, h in zip((2, 0), half)
        ]
        lo[n] = o23
        return apply_map(o01, lp[n, 0], o23)

    row_i = lax.broadcasted_iota(jnp.int32, (B, 2 * B), 0)
    col_i = lax.broadcasted_iota(jnp.int32, (B, 2 * B), 1)
    unit = jnp.where(row_i == col_i, 1.0, 0.0).astype(F32)

    def later(ref, out, n):
        o, p = combine((ref[1, 0], ref[1, 1]), (lo[n], lp[n, 1]))
        out[0, 0] = o
        out[0, 1] = p
        out[1, 0] = lo[n]
        out[1, 1] = lp[n, 1]
        out[2] = ref[3]
        out[3, 0] = zero
        out[3, 1] = unit

    zcopy = remote(zbuf, zrecv, z_sem.at[0], z_sem.at[1], (zpeer, e))

    prepare(0)
    xp.finish()
    level_p(xs, 0)
    ys[y, 1] = prod(lp[0, 0], lp[0, 1])
    yp.start()
    prepare(1)
    xo.forward()
    prepare(2)
    yp.forward()
    prepare(3)
    xo.finish()
    ys[y, 0] = level_o(xs, 0)
    yo.start()
    yp.finish()
    level_p(ys, 1)
    later(xs, ex, 0)
    o, p = combine((tbuf[1, 0], tbuf[1, 1]), (ex[x, 0], ex[x, 1]))
    maps[0, 0] = ex[x, 0]
    maps[0, 1] = ex[x, 1]
    maps[1, 0] = o
    maps[1, 1] = p
    for i in range(4, EARLY):
        prepare(i)
    yo.forward()
    ey[0, 1] = prod(ys[1, 1], lp[1, 1])
    ey[1, 1] = lp[1, 1]
    ey[2, 1] = ys[3, 1]
    ey[3, 1] = unit
    ly = [lhs(maps[n, 1]) for n in range(2)]
    ry = rhs(ey[y, 1])
    for n in range(2):
        mp[n] = mul(ly[n], ry)
    yo.finish()
    zbuf[...] = level_o(ys, 1)

    @pl.when(z == 1)
    def _():
        zcopy.start()

    ey[0, 0] = apply_map(ys[1, 0], ys[1, 1], lo[1])
    ey[1, 0] = lo[1]
    ey[2, 0] = ys[3, 0]
    ey[3, 0] = zero
    ry = rhs(ey[y, 0])
    half = [mul(lhs(maps[n, 1]), ry) for n in range(2)]
    for n in range(2):
        maps[n, 0] += mul(lhs(half[n]), rhs_t(maps[n, 1]), True)

    give, keep = core, 1 - core

    @pl.when(z == 1)
    def _():
        dbuf[...] = maps[give, 0]
        xin[core] = maps[keep, 0]

    @pl.when(z == 0)
    def _():
        prepare(EARLY)
        zcopy.wait_recv()
        dbuf[...] = apply_map(maps[give, 0], mp[give], zrecv[...])

    down = remote(dbuf, xin.at[core], d_sem.at[0], d_sem.at[1], (partner, e))
    down.start()

    @pl.when(z == 0)
    def _():
        xin[core] = apply_map(maps[keep, 0], mp[keep], zrecv[...])

    def weigh(i, k):
        zk = mul(q[i, k], (xt[k, 0], xt[k, 1]))
        w[i, k] = w0[i, k] + mul(lhs(zk), rhs_t(gg[i, k]), True)

    def first_weights(n, carry):
        k = jnp.where(n == 0, core, 1 - core)

        @pl.when(n == 1)
        def _():
            down.wait_recv()

        high, low = rhs(xin[k])
        xt[k, 0] = high
        xt[k, 1] = low
        weigh(0, k)
        return carry

    lax.fori_loop(0, 2, first_weights, 0)
    halo = remote(w.at[0], w.at[S], h_sem.at[0], h_sem.at[1], (prev, e))

    @pl.when(s > 0)
    def _():
        halo.start()


    def spread(i, n):
        return remote(
            (up, down_rows)[n].at[i], (from_below, from_above)[n].at[i],
            r_send.at[i, n], r_recv.at[i, n], (s, epeer((1, 3)[n])),
        )

    def pass_on(pair_no, kind):
        at = pl.ds(2 * pair_no, 2)
        return remote(
            mid.at[kind, at], passed.at[kind, at],
            p_send.at[pair_no, kind], p_recv.at[pair_no, kind], (s, epeer((3, 1)[kind])),
        )

    def rows_of(kind, d):
        return stage[kind, pl.ds(pl.multiple_of(epeer(d) * ROWS, ROWS), ROWS)]

    def pass_step(pair_no, carry):
        for m in range(2):
            i = 2 * pair_no + m
            for n in range(2):
                spread(i, n).wait_recv()
            mid[0, i] += from_above[i, 0]
            mid[1, i] += from_below[i, 1]
        for kind in range(2):
            pass_on(pair_no, kind).start()
        return carry

    def finals(i):
        stage[0] = w[i, 0, :, 0:B] + w[i, 1, :, 0:B]
        if i + 1 == EARLY:

            @pl.when(z == 1)
            def _():
                prepare(EARLY)

        elif EARLY < i + 1 < S:
            prepare(i + 1)
        if i < S - 1:
            zs = [mul(q[i + 1, k], (xt[k, 0], xt[k, 1])) for k in range(2)]
            for k in range(2):
                w[i + 1, k] = w0[i + 1, k] + mul(lhs(zs[k]), rhs_t(gg[i + 1, k]), True)
        else:

            @pl.when(s < slabs - 1)
            def _():
                halo.wait_recv()

            @pl.when(last)
            def _():
                for k in range(2):
                    w[S, k] = zero

        nts, nns = [], []
        for k in range(2):
            wh, wl = split(w[i + 1, k])
            nts.append(jnp.concatenate([wh, wl], 0))
            for m in (0, B):
                nns.append(jnp.concatenate([wh[:, m : m + B], wl[:, m : m + B]], 1))
        t = dot(
            jnp.concatenate([vv[i, 0, 0], vv[i, 0, 1]], 1), jnp.concatenate(nts, 1), True
        ) + dot(jnp.concatenate([vv[i, 1, 0], vv[i, 1, 1]], 1), jnp.concatenate(nns, 0))
        stage[1] = t[:B, :B] + (t[:B, B:] + t[B:, :B])
        up[i, 0] = rows_of(0, 1)
        up[i, 1] = rows_of(1, 2)
        down_rows[i, 0] = rows_of(0, 2)
        down_rows[i, 1] = rows_of(1, 3)
        for n in range(2):
            spread(i, n).start()
        mid[0, i] = rows_of(0, 3)
        mid[1, i] = rows_of(1, 1)
        for kind in range(2):
            kept[i, kind] = rows_of(kind, 0)

    for i in range(S):
        finals(i)
        if i in RELAY_AT:
            pass_step(RELAY_AT.index(i), 0)
    lax.fori_loop(len(RELAY_AT), S // 2, pass_step, 0)

    def collect(pair_no, carry):
        for kind in range(2):
            pass_on(pair_no, kind).wait_recv()
        for m in range(2):
            i = 2 * pair_no + m
            on_ref[i] = kept[i, 0] + from_below[i, 0] + passed[0, i]
            cp_ref[i] = kept[i, 1] + from_above[i, 1] + passed[1, i]
        return carry

    lax.fori_loop(0, S // 2, collect, 0)

    for t in range(2):
        pair(t).wait_send()
    for ring in (xp, xo, yp, yo):
        ring.drain()

    @pl.when(z == 1)
    def _():
        zcopy.wait_send()

    down.wait_send()

    @pl.when(s > 0)
    def _():
        halo.wait_send()

    def drain(i, carry):
        for n in range(2):
            spread(2 * i, n).wait_send()
            spread(2 * i + 1, n).wait_send()
            pass_on(i, n).wait_send()
        return carry

    lax.fori_loop(0, S // 2, drain, 0)


def on_device(green_blocks, couplings, green_cotangent):
    shape = (S, 2, 2, B, B)
    block = (B, 2 * B)
    vmem = pltpu.VMEM
    out = jax.ShapeDtypeStruct((S, ROWS, B), F32)
    dma = pltpu.SemaphoreType.DMA
    return pl.pallas_call(
        kernel,
        out_shape=(out, out),
        in_specs=[pl.BlockSpec(memory_space=pl.ANY)] * 3,
        out_specs=(pl.BlockSpec(memory_space=vmem),) * 2,
        scratch_shapes=[
            vmem(shape, F32),
            vmem((S, B, B), F32),
            vmem(shape, F32),
            vmem((S, 2) + block, F32),
            vmem((2,) + block, F32),
            vmem((2, 2) + block, F32),
            vmem((2, 2) + block, F32),
            vmem((NX, 2) + block, F32),
            vmem((NY, 2) + block, F32),
            vmem((NX, 2) + block, F32),
            vmem((NY, 2) + block, F32),
            vmem((2, 2) + block, F32),
            vmem((2,) + block, F32),
            vmem(block, F32),
            vmem(block, F32),
            vmem(block, F32),
            vmem((2,) + block, F32),
            vmem((S, 2, 2) + block, F32),
            vmem((2, 2) + block, F32),
            vmem((2,) + block, F32),
            vmem((S, 2) + block, F32),
            vmem((S, 2, 2 * B, 2 * B), BF16),
            vmem((S, 2) + block, F32),
            vmem((S, 2, 2, 2 * B, 2 * B), BF16),
            vmem((2, 2, 2 * B, 2 * B), BF16),
            vmem((S + 1, 2) + block, F32),
            vmem((2, B, B), F32),
            vmem((S, 2, ROWS, B), F32),
            vmem((S, 2, ROWS, B), F32),
            vmem((2, S, ROWS, B), F32),
            vmem((S, 2, ROWS, B), F32),
            vmem((S, 2, ROWS, B), F32),
            vmem((S, 2, ROWS, B), F32),
            vmem((2, S, ROWS, B), F32),
            dma((S,)),
            dma((S,)),
            dma,
            dma((2, 2)),
            dma((2, 6)),
            dma((2, 6)),
            dma((2, 6)),
            dma((2, 6)),
            dma((2,)),
            dma((2,)),
            dma((2,)),
            dma((S, 2)),
            dma((S, 2)),
            dma((S // 2, 2)),
            dma((S // 2, 2)),
        ],
        compiler_params=pltpu.CompilerParams(
            collective_id=0, has_side_effects=True, vmem_limit_bytes=62 * 1024 * 1024
        ),
    )(
        green_blocks.reshape(shape),
        couplings,
        green_cotangent.reshape(shape),
    )


def solution(mesh):
    in_specs = (
        P("slab", "energy", None, None, None, None),
        P("slab", None, None),
        P("slab", "energy", None, None, None, None),
    )
    out_specs = (P("slab", "energy", None), P("slab", "energy", None))
    return jax.shard_map(
        on_device, mesh=mesh, in_specs=in_specs, out_specs=out_specs, check_vma=False
    )
```
